32 devices in a mesh: rep: 2 (over x), tp: 16 (over z, y, core).
Axes of the slice: x: 2, y: 2, z: 4, core: 2. Of those that a mesh axis runs over, the one named last changes fastest.
Arguments:
- tokens: bfloat16 [512, 8192], P(('rep', 'tp')), parts along dimension 0, may hold values from -6 to 6
- cotangent: bfloat16 [10240, 512], P('tp', 'rep'), parts along dimension 1, may hold values from -6 to 6
- joined_weight: bfloat16 [10240, 8192], P('tp'), may hold values from -0.0625 to 0.0625
- adapter_down_maps: bfloat16 [64, 16, 8192], P(None, None, 'tp'), may hold values from -0.0625 to 0.0625
- adapter_up_maps: bfloat16 [10240, 1024], P('tp'), may hold values from -0.0625 to 0.0625
- adapter_token_lengths: int32 [128], P('rep'), parts along dimension 0, may hold values from 1 to 16, 256 in all
- adapter_storage_slot: int32 [64], replicated, may hold values from 0 to 63, each once
Outputs:
- grad_tokens: bfloat16 [512, 8192], P(('rep', 'tp')), parts along dimension 0
- down_map_gradient: float32 [128, 16, 8192], P('rep', None, 'tp'), parts along dimension 0
- up_map_gradient: float32 [10240, 2048], P('tp', 'rep'), parts along dimension 1
The draws below stay inside these ranges and needn't reach their ends.
There are 2 independent parts, one for each index of `rep`. The reference program is written for one: setup_inputs(seed, part) draws one part's arguments, and reference() takes and returns one part's arrays. A program takes and returns all parts, laid end to end along the dimension named above; an argument that names none is the same for every part. Nothing has to cross between parts.
Inputs may be any that keep to these rules, and one draw needn't show every extreme that they name: `adapter_token_lengths`: they sum to 256; tokens are ordered by adapter. `adapter_storage_slot`: A permutation.
All inputs are finite; a program needn't handle non-finite values.
Results may differ from the reference program's by a relative error of at most 0.0051.
Values may be sent and summed in bfloat16 or wider, within the bound.
No kernel may reach another device: no remote copies, remote signals or barrier semaphores. Data moves between devices by JAX's collectives and lax.ppermute only.
A program may use at most 128 MiB of HBM per device.

```python
import math
import jax
import jax.numpy as jnp
import numpy as np
from jax import lax

MODEL_WIDTH = 8192
JOINED_COLUMNS = 10240
ADAPTER_RANK = 16
ADAPTER_COUNT = 64
TOKENS = 256
MOST = 16


def level_of(rng, dims, pieces, least, high):
    def one(dim, parts):
        draws = jax.random.uniform(jax.random.fold_in(jax.random.fold_in(rng, 6), dim), (parts,), jnp.float32, least / len(pieces), high / len(pieces))
        return jnp.repeat(jnp.exp(draws), dims[dim] // parts).reshape((-1,) + (1,) * (len(dims) - dim - 1))

    level = one(*pieces[0])
    for cut in pieces[1:]:
        level = level * one(*cut)
    return level


def profile(number_of, total, reach, lean):
    weights = [(1 << 20) // math.isqrt(standing ** lean) + 1 for standing in range(2, number_of + 1)]
    spare, holding = total - reach - (number_of - 1), [1] * (number_of - 1)
    while spare > 0:
        free = [i for i in range(number_of - 1) if holding[i] < reach]
        mass, remaining = sum([weights[i] for i in free]), spare
        for i in free:
            addition = min(reach - holding[i], max(1, remaining * weights[i] // mass), spare)
            holding[i] = holding[i] + addition
            spare = spare - addition
    return np.array([reach] + holding)


def uneven(key, amount, total, bound, slope):
    if amount == 2:
        one = jax.random.randint(key, (), max(1, total - bound), min(bound, total - 1) + 1)
        return jnp.stack([one, total - one])
    sizes = jnp.asarray(profile(amount, total, bound, slope), jnp.int32)
    couples = (amount - 1) // 2
    source_of, taker = sizes[1:1 + 2 * couples:2], sizes[2:2 + 2 * couples:2]
    margin = jnp.minimum(source_of - 1, bound - taker)
    shifted = jax.random.randint(jax.random.fold_in(key, 1), (couples,), 0, 1 << 20) % (margin + 1)
    sizes = sizes.at[1:1 + 2 * couples:2].set(source_of - shifted).at[2:2 + 2 * couples:2].set(taker + shifted)
    return sizes[jax.random.permutation(jax.random.fold_in(key, 2), amount)]


def noise(key, dims, spread, reach, shards=(), held_as=jnp.bfloat16):
    factor_of = level_of(key, dims, shards, -0.22, 0.18) if shards else 1.0
    result = jax.random.normal(key, dims, jnp.float32) * spread * factor_of
    return jnp.minimum(jnp.maximum(result, -reach), reach).astype(held_as)


def setup_inputs(seed: int = 0, part: int = 0) -> dict:
    streams_of = jax.random.split(jax.random.key(seed), 8)
    part_keys = jax.random.split(jax.random.fold_in(streams_of[7], part), 8)
    tokens = noise(part_keys[0], (TOKENS, MODEL_WIDTH), 1.0, 6.0, ((0, 16),))
    cotangent = noise(part_keys[1], (JOINED_COLUMNS, TOKENS), 1.0, 6.0, ((0, 16),))
    joined_weight = noise(streams_of[2], (JOINED_COLUMNS, MODEL_WIDTH), MODEL_WIDTH ** -0.5, 0.0625, ((0, 16),))
    adapter_down_maps = noise(streams_of[3], (ADAPTER_COUNT, ADAPTER_RANK, MODEL_WIDTH), MODEL_WIDTH ** -0.5, 0.0625, ((2, 16),))
    adapter_up_maps = noise(streams_of[4], (JOINED_COLUMNS, ADAPTER_COUNT * ADAPTER_RANK), JOINED_COLUMNS ** -0.5, 0.0625, ((0, 16),))
    adapter_token_lengths = uneven(part_keys[5], ADAPTER_COUNT, TOKENS, MOST, 2).astype(jnp.int32)
    adapter_storage_slot = jax.random.permutation(streams_of[6], ADAPTER_COUNT).astype(jnp.int32)
    return {"tokens": tokens, "cotangent": cotangent, "joined_weight": joined_weight, "adapter_down_maps": adapter_down_maps, "adapter_up_maps": adapter_up_maps, "adapter_token_lengths": adapter_token_lengths, "adapter_storage_slot": adapter_storage_slot}


ADAPTER_SCALE = 2.0
eps = 1e-06

def reference(tokens, cotangent, joined_weight, adapter_down_maps, adapter_up_maps, adapter_token_lengths, adapter_storage_slot):
    contract_token_rows = (((0,), (0,)), ((), ()))
    seg_ends = jnp.cumsum(adapter_token_lengths).astype(jnp.int32)
    starts = seg_ends - adapter_token_lengths
    position = jnp.arange(TOKENS, dtype=jnp.int32)[:, None]
    member = ((position >= starts[None, :]) & (position < seg_ends[None, :])).astype(jnp.float32)
    permuted = (adapter_storage_slot[:, None] == jnp.arange(ADAPTER_COUNT, dtype=jnp.int32)[None, :]).astype(jnp.float32)
    chosen = jnp.dot(member, permuted, precision=lax.Precision.HIGHEST)
    wide_sel = jnp.repeat(chosen, ADAPTER_RANK, axis=1)
    fold_rows = (jnp.arange(ADAPTER_COUNT * ADAPTER_RANK, dtype=jnp.int32)[:, None] % ADAPTER_RANK == jnp.arange(ADAPTER_RANK, dtype=jnp.int32)[None, :]).astype(jnp.float32)
    as_float = tokens.astype(jnp.float32)
    inv_rms = lax.rsqrt(lax.optimization_barrier(jnp.mean(as_float * as_float, axis=1, keepdims=True)) + eps)
    normed = as_float * inv_rms
    normed_halfwidth = normed.astype(jnp.bfloat16)
    down_flattened = adapter_down_maps.reshape(ADAPTER_COUNT * ADAPTER_RANK, MODEL_WIDTH)
    down_all = jnp.dot(normed_halfwidth, down_flattened.T, preferred_element_type=jnp.float32)
    up_every_slot = lax.dot_general(cotangent, adapter_up_maps, contract_token_rows, preferred_element_type=jnp.float32)
    low_sum = jnp.dot(down_all * wide_sel, fold_rows, precision=lax.Precision.HIGHEST)
    back_sum = jnp.dot(up_every_slot * wide_sel, fold_rows, precision=lax.Precision.HIGHEST)
    low_bf = low_sum.astype(jnp.bfloat16)
    back_bf = back_sum.astype(jnp.bfloat16)
    left_projected = (wide_sel * jnp.tile(low_bf.astype(jnp.float32), (1, ADAPTER_COUNT))).astype(jnp.bfloat16)
    left_gradient = (wide_sel * jnp.tile(back_bf.astype(jnp.float32), (1, ADAPTER_COUNT))).astype(jnp.bfloat16)
    up_map_gradient = ADAPTER_SCALE * jnp.dot(cotangent, left_projected, preferred_element_type=jnp.float32)
    down_map_gradient = ADAPTER_SCALE * jnp.dot(left_gradient.T, normed_halfwidth, preferred_element_type=jnp.float32)
    down_map_gradient = down_map_gradient.reshape(ADAPTER_COUNT, ADAPTER_RANK, MODEL_WIDTH)
    adapter_term = ADAPTER_SCALE * jnp.dot(left_gradient, down_flattened, preferred_element_type=jnp.float32)
    frozen_term = lax.dot_general(cotangent, joined_weight, contract_token_rows, preferred_element_type=jnp.float32)
    normed_gradient = frozen_term + adapter_term
    mean_term = lax.optimization_barrier(jnp.mean(normed_gradient * normed, axis=1, keepdims=True))
    grad_tokens = (inv_rms * (normed_gradient - normed * mean_term)).astype(jnp.bfloat16)
    return (grad_tokens, down_map_gradient, up_map_gradient)
```

```python
import functools

import jax
import jax.numpy as jnp
from jax import lax
from jax.experimental import pallas as pl
from jax.experimental.pallas import tpu as pltpu
from jax.sharding import PartitionSpec as P

SCALE = 2.0
EPS = 1e-06
BF = jnp.bfloat16
F32 = jnp.float32
NT = (((1,), (1,)), ((), ()))
TN = (((0,), (0,)), ((), ()))
VMEM = pl.BlockSpec(memory_space=pltpu.VMEM)
SMEM = pl.BlockSpec(memory_space=pltpu.SMEM)


def stages_of(tp):
    bits = [1 << b for b in range(tp.bit_length() - 1)]
    groups = [bits[:1], bits[1:2]]
    rest = bits[2:]
    groups += [rest[i : i + 2] for i in range(0, len(rest), 2)]
    stages = []
    for group in groups:
        masks = [0]
        for b in group:
            masks = masks + [m | b for m in masks]
        if len(masks) > 1:
            stages.append(masks)
    return stages


def block_order(stages):
    order = [0]
    for masks in stages:
        order = [o | m for o in order for m in masks]
    return order


def iota(shape, dim):
    return lax.broadcasted_iota(jnp.int32, shape, dim)


def membership(lens_ref, slots_ref, rows):
    count = lens_ref.shape[1]
    lens = jnp.broadcast_to(lens_ref[...].astype(F32), (8, count)).astype(BF)
    upto = (iota((count, count), 0) <= iota((count, count), 1)).astype(F32).astype(BF)
    ends = jnp.dot(lens, upto, preferred_element_type=F32)[:1].astype(jnp.int32)
    starts = ends - lens_ref[...]
    position = iota((rows, count), 0)
    member = ((position >= starts) & (position < ends)).astype(F32).astype(BF)
    match = (iota((count, count), 0) == slots_ref[...]).astype(F32).astype(BF)
    return member, match


def mask_by_column(lens_ref, slots_ref, rows, rank):
    member, match = membership(lens_ref, slots_ref, rows)
    chosen = lax.dot_general(match, member, NT, preferred_element_type=F32).astype(BF)
    slots = match.shape[0]
    wide = (iota((slots * rank, slots), 0) // rank == iota((slots * rank, slots), 1)).astype(F32).astype(BF)
    return jnp.dot(wide, chosen, preferred_element_type=F32)


def prep_kernel(order, rank, me_ref, lens_ref, slots_ref, tok_ref, cot_ref, up_ref, send_ref, cotp_ref, cott):
    tp, own, _ = send_ref.shape
    width = tok_ref.shape[1]
    share = width // tp
    rows, _ = cott.shape
    cott[...] = cot_ref[...].astype(F32).T.astype(BF)
    tok = tok_ref[...].astype(F32)
    inv = lax.rsqrt(jnp.mean(tok * tok, axis=1, keepdims=True) + EPS)
    normed = (tok * inv).astype(BF)
    member, match = membership(lens_ref, slots_ref, rows)
    chosen = lax.dot_general(member, match, NT, preferred_element_type=F32).astype(BF)
    slots = match.shape[0]
    wide = (iota((slots, slots * rank), 1) // rank == iota((slots, slots * rank), 0)).astype(F32).astype(BF)
    mask = jnp.dot(chosen, wide, preferred_element_type=F32)
    every = jnp.dot(cott[...], up_ref[...], preferred_element_type=F32) * mask
    lanes = every[:, :128]
    for i in range(1, slots * rank // 128):
        lanes = lanes + every[:, i * 128 : (i + 1) * 128]
    turned = lanes.T
    back = turned[:rank]
    for i in range(1, 128 // rank):
        back = back + turned[i * rank : (i + 1) * rank]
    back = back.astype(BF)
    for q in range(tp):
        send_ref[q, :, :share] = normed[:, q * share : (q + 1) * share]
        send_ref[q, :, share:] = back
    me = me_ref[0]
    for i, mask_bits in enumerate(order):
        source = pl.multiple_of((me ^ mask_bits) * own, own)
        cotp_ref[pl.ds(i * own, own), :] = cott[pl.ds(source, own), :]


def product_kernel(cotp_ref, weight_ref, *parts):
    out = jnp.dot(cotp_ref[...], weight_ref[...], preferred_element_type=F32)
    each = parts[0].shape[0]
    for i, part in enumerate(parts):
        part[...] = out[i * each : (i + 1) * each].astype(BF)


def middle_kernel(rank, lens_ref, slots_ref, recv_ref, down_ref, send_ref, left_ref):
    tp, own, wide = recv_ref.shape
    rows = tp * own
    share = wide - rows
    mask = mask_by_column(lens_ref, slots_ref, rows, rank)
    normed = recv_ref[:, :, :share].reshape(rows, share)
    every = lax.dot_general(down_ref[...], normed, NT, preferred_element_type=F32) * mask
    slots = every.shape[0] // rank
    low = jnp.sum(every.reshape(slots, rank, rows), axis=0).astype(BF)
    back = jnp.sum(recv_ref[:, :, share:].astype(F32), axis=0).astype(BF).astype(F32)
    left = (mask.reshape(slots, rank, rows) * back[None]).reshape(slots * rank, rows).astype(BF)
    left_ref[...] = left
    term = SCALE * lax.dot_general(left, down_ref[...], TN, preferred_element_type=F32)
    send_ref[:, :, :share] = term.astype(BF).reshape(tp, own, share)
    for q in range(tp):
        send_ref[q, :, share:] = low


def down_kernel(left_ref, recv_ref, out_ref):
    tp, own, wide = recv_ref.shape
    rows = tp * own
    share = wide - rows
    normed = recv_ref[:, :, :share].reshape(rows, share)
    out_ref[...] = SCALE * jnp.dot(left_ref[...], normed, preferred_element_type=F32)


def up_kernel(rank, lens_ref, slots_ref, recv_ref, cot_ref, out_ref):
    tp, own, wide = recv_ref.shape
    rows = tp * own
    share = wide - rows
    mask = mask_by_column(lens_ref, slots_ref, rows, rank)
    slots = mask.shape[0] // rank
    low = jnp.sum(recv_ref[:, :, share:].astype(F32), axis=0).astype(BF).astype(F32)
    left = (mask.reshape(slots, rank, rows) * low[None]).reshape(slots * rank, rows).astype(BF)
    out_ref[...] = SCALE * lax.dot_general(cot_ref[...], left, NT, preferred_element_type=F32)


def final_kernel(pieces, recv_ref, tok_ref, *refs):
    out_ref = refs[-1]
    tp, own, _ = recv_ref.shape
    width = tok_ref.shape[1]
    share = width // tp
    chunks = []
    at = 0
    for n in pieces:
        total = refs[at][...].astype(F32)
        for r in refs[at + 1 : at + n]:
            total = total + r[...].astype(F32)
        at += n
        chunks.append(total)
    term = jnp.concatenate([recv_ref[q, :, :share].astype(F32) for q in range(tp)], axis=1)
    grad = jnp.concatenate(chunks, axis=1) + term
    tok = tok_ref[...].astype(F32)
    inv = lax.rsqrt(jnp.mean(tok * tok, axis=1, keepdims=True) + EPS)
    normed = tok * inv
    mean = jnp.mean(grad * normed, axis=1, keepdims=True)
    out_ref[...] = (inv * (grad - normed * mean)).astype(BF)


def call(kernel, out, n_in, smem=(), scratch=(), flops=0, nbytes=0, vmem=48):
    return pl.pallas_call(
        kernel,
        out_shape=out,
        in_specs=[SMEM if i in smem else VMEM for i in range(n_in)],
        out_specs=jax.tree.map(lambda _: VMEM, out),
        scratch_shapes=list(scratch),
        cost_estimate=pl.CostEstimate(flops=int(flops), bytes_accessed=int(nbytes), transcendentals=0),
        compiler_params=pltpu.CompilerParams(vmem_limit_bytes=vmem << 20),
    )


def shape(dims, dtype=BF):
    return jax.ShapeDtypeStruct(dims, dtype)


def body(tokens, cotangent, weight, down_maps, up_maps, lengths, slots):
    tp = lax.axis_size("tp")
    me = lax.axis_index("tp").reshape(1)
    own, width = tokens.shape
    rows = own * tp
    count, rank, share = down_maps.shape
    columns = cotangent.shape[0]
    stages = stages_of(tp)
    order = block_order(stages)
    lens = lengths.reshape(1, count)
    slot = slots.reshape(1, count)
    down_flat = down_maps.reshape(count * rank, share)

    send, cotp = call(
        functools.partial(prep_kernel, order, rank),
        (shape((tp, own, share + rows)), shape((rows, columns))),
        6,
        smem=(0,),
        scratch=[pltpu.VMEM((rows, columns), BF)],
        flops=2 * rows * columns * count * rank,
        nbytes=3 << 20,
    )(me, lens, slot, tokens, cotangent, up_maps)
    recv = lax.all_to_all(send, "tp", split_axis=0, concat_axis=0, tiled=True)

    def product(first, size):
        block = 1024
        m = len(stages[0])
        each = rows // m
        return pl.pallas_call(
            product_kernel,
            grid=(size // block,),
            out_shape=[shape((each, size))] * m,
            in_specs=[
                pl.BlockSpec((rows, columns), lambda i: (0, 0)),
                pl.BlockSpec((columns, block), lambda i: (0, first // block + i)),
            ],
            out_specs=[pl.BlockSpec((each, block), lambda i: (0, i))] * m,
            cost_estimate=pl.CostEstimate(
                flops=2 * rows * columns * size,
                bytes_accessed=2 * columns * size + 2 * rows * size,
                transcendentals=0,
            ),
            compiler_params=pltpu.CompilerParams(vmem_limit_bytes=32 << 20),
        )(cotp, weight)

    def pairs(m):
        return [(i, i ^ m) for i in range(tp)]

    def scatter(parts):
        for s, masks in enumerate(stages):
            got = [lax.ppermute(part, "tp", pairs(m)) for m, part in zip(masks[1:], parts[1:])]
            if s == len(stages) - 1:
                return [parts[0]] + got
            m = len(stages[s + 1])
            each = parts[0].shape[0] // m
            new = []
            for i in range(m):
                total = parts[0][i * each : (i + 1) * each].astype(F32)
                for g in got:
                    total = total + g[i * each : (i + 1) * each].astype(F32)
                new.append(total.astype(BF))
            parts = new

    sizes = [width // 2, width // 2]
    chunks = []
    first = 0
    for size in sizes:
        chunks.append(scatter(product(first, size)))
        first += size

    send2, left = call(
        functools.partial(middle_kernel, rank),
        (shape((tp, own, share + rows)), shape((count * rank, rows))),
        4,
        flops=4 * rows * share * count * rank,
        nbytes=3 << 20,
    )(lens, slot, recv, down_flat)
    recv2 = lax.all_to_all(send2, "tp", split_axis=0, concat_axis=0, tiled=True)
    down_grad = call(
        down_kernel, shape((count * rank, share), F32), 2, flops=2 * rows * share * count * rank, nbytes=3 << 20
    )(left, recv)
    up_grad = call(
        functools.partial(up_kernel, rank),
        shape((columns, count * rank), F32),
        4,
        flops=2 * rows * columns * count * rank,
        nbytes=3 << 20,
    )(lens, slot, recv2, cotangent)
    flat = [piece for chunk in chunks for piece in chunk]
    grad_tokens = call(
        functools.partial(final_kernel, [len(c) for c in chunks]), shape((own, width)), 2 + len(flat), nbytes=2 << 20
    )(recv2, tokens, *flat)
    return grad_tokens, down_grad.reshape(count, rank, share), up_grad


def solution(mesh):
    in_specs = (
        P(("rep", "tp"), None),
        P("tp", "rep"),
        P("tp", None),
        P(None, None, "tp"),
        P("tp", None),
        P("rep"),
        P(),
    )
    out_specs = (P(("rep", "tp"), None), P("rep", None, "tp"), P("tp", "rep"))
    return jax.shard_map(body, mesh=mesh, in_specs=in_specs, out_specs=out_specs, check_vma=False)
```

```python
import functools

import jax
import jax.numpy as jnp
from jax import lax
from jax.experimental import pallas as pl
from jax.experimental.pallas import tpu as pltpu
from jax.sharding import PartitionSpec as P

SCALE = 2.0
EPS = 1e-06
BF = jnp.bfloat16
F32 = jnp.float32
NT = (((1,), (1,)), ((), ()))
TN = (((0,), (0,)), ((), ()))
VMEM = pl.BlockSpec(memory_space=pltpu.VMEM)
SMEM = pl.BlockSpec(memory_space=pltpu.SMEM)


def stages_of(tp):
    bits = [1 << b for b in range(tp.bit_length() - 1)]
    groups = [bits[:1], bits[1:2]]
    rest = bits[2:]
    groups += [rest[i : i + 2] for i in range(0, len(rest), 2)]
    stages = []
    for group in groups:
        masks = [0]
        for b in group:
            masks = masks + [m | b for m in masks]
        if len(masks) > 1:
            stages.append(masks)
    return stages


def block_order(stages):
    order = [0]
    for masks in stages:
        order = [o | m for o in order for m in masks]
    return order


def iota(shape, dim):
    return lax.broadcasted_iota(jnp.int32, shape, dim)


def membership(lens_ref, slots_ref, rows):
    count = lens_ref.shape[1]
    lens = jnp.broadcast_to(lens_ref[...].astype(F32), (8, count)).astype(BF)
    upto = (iota((count, count), 0) <= iota((count, count), 1)).astype(F32).astype(BF)
    ends = jnp.dot(lens, upto, preferred_element_type=F32)[:1].astype(jnp.int32)
    starts = ends - lens_ref[...]
    position = iota((rows, count), 0)
    member = ((position >= starts) & (position < ends)).astype(F32).astype(BF)
    match = (iota((count, count), 0) == slots_ref[...]).astype(F32).astype(BF)
    return member, match


def mask_by_column(lens_ref, slots_ref, rows, rank):
    member, match = membership(lens_ref, slots_ref, rows)
    chosen = lax.dot_general(match, member, NT, preferred_element_type=F32).astype(BF)
    slots = match.shape[0]
    wide = (iota((slots * rank, slots), 0) // rank == iota((slots * rank, slots), 1)).astype(F32).astype(BF)
    return jnp.dot(wide, chosen, preferred_element_type=F32)


def cast_parts(out, parts):
    each = parts[0].shape[0]
    for i, part in enumerate(parts):
        part[...] = out[i * each : (i + 1) * each].astype(BF)


def fetch_weight(weight_hbm, wbuf, sems, first, block):
    copies = []
    for i in range(wbuf.shape[1] // block):
        copies.append(
            pltpu.make_async_copy(
                weight_hbm.at[:, pl.ds(first + i * block, block)], wbuf.at[:, pl.ds(i * block, block)], sems.at[i]
            )
        )
    return copies


def multiply(cotp, wbuf, copies, block, parts):
    each = parts[0].shape[0]
    for i, copy in enumerate(copies):
        copy.wait()
        columns = pl.ds(i * block, block)
        out = jnp.dot(cotp, wbuf[:, columns], preferred_element_type=F32)
        for k, part in enumerate(parts):
            part[:, columns] = out[k * each : (k + 1) * each].astype(BF)


def first_kernel(order, own, block, me_ref, cot_hbm, weight_hbm, cotp_ref, *refs):
    *parts, cot, cott, wbuf, sem, sems = refs
    cot_copy = pltpu.make_async_copy(cot_hbm, cot, sem)
    cot_copy.start()
    copies = fetch_weight(weight_hbm, wbuf, sems, 0, block)
    for copy in copies:
        copy.start()
    cot_copy.wait()
    cott[...] = cot[...].astype(F32).T.astype(BF)
    me = me_ref[0]
    for i, mask_bits in enumerate(order):
        source = pl.multiple_of((me ^ mask_bits) * own, own)
        cotp_ref[pl.ds(i * own, own), :] = cott[pl.ds(source, own), :]
    multiply(cotp_ref[...], wbuf, copies, block, parts)


def second_kernel(order, rank, first, block, me_ref, lens_ref, slots_ref, cotp_ref, tok_hbm, up_hbm, weight_hbm, send_ref, *refs):
    *parts, tokv, up, wbuf, back_rows, sem, sems = refs
    tp, own, _ = send_ref.shape
    width = tokv.shape[1]
    share = width // tp
    rows = cotp_ref.shape[0]
    tok_copy = pltpu.make_async_copy(tok_hbm, tokv, sem.at[0])
    tok_copy.start()
    up_copy = pltpu.make_async_copy(up_hbm, up, sem.at[1])
    up_copy.start()
    copies = fetch_weight(weight_hbm, wbuf, sems, first, block)
    for copy in copies:
        copy.start()
    member, match = membership(lens_ref, slots_ref, rows)
    chosen = lax.dot_general(member, match, NT, preferred_element_type=F32).astype(BF)
    slots = match.shape[0]
    wide = (iota((slots, slots * rank), 1) // rank == iota((slots, slots * rank), 0)).astype(F32).astype(BF)
    mask = jnp.dot(chosen, wide, preferred_element_type=F32)
    me = me_ref[0]
    tok_copy.wait()
    tok = tokv[...].astype(F32)
    inv = lax.rsqrt(jnp.mean(tok * tok, axis=1, keepdims=True) + EPS)
    normed = (tok * inv).astype(BF)
    up_copy.wait()
    every = jnp.dot(cotp_ref[...], up[...], preferred_element_type=F32)
    for i, mask_bits in enumerate(order):
        target = pl.multiple_of((me ^ mask_bits) * own, own)
        back_rows[pl.ds(target, own), :] = every[i * own : (i + 1) * own]
    every = back_rows[...] * mask
    lanes = every[:, :128]
    for i in range(1, slots * rank // 128):
        lanes = lanes + every[:, i * 128 : (i + 1) * 128]
    turned = lanes.T
    back = turned[:rank]
    for i in range(1, 128 // rank):
        back = back + turned[i * rank : (i + 1) * rank]
    back = back.astype(BF)
    for q in range(tp):
        send_ref[q, :, :share] = normed[:, q * share : (q + 1) * share]
        send_ref[q, :, share:] = back
    multiply(cotp_ref[...], wbuf, copies, block, parts)


def total_of(refs, i, each):
    total = refs[0][i * each : (i + 1) * each].astype(F32)
    for r in refs[1:]:
        total = total + r[i * each : (i + 1) * each].astype(F32)
    return total.astype(BF)


def sum_kernel(groups, passed, *refs):
    n_in = sum(t for t, _ in groups)
    terms, outs = refs[: n_in], refs[n_in + passed :]
    at, to = 0, 0
    for n, m in groups:
        each = terms[at].shape[0] // m
        for i in range(m):
            outs[to + i][...] = total_of(terms[at : at + n], i, each)
        at, to = at + n, to + m


def middle_kernel(rank, lens_ref, slots_ref, recv_ref, down_ref, send_ref, left_ref):
    tp, own, wide = recv_ref.shape
    rows = tp * own
    share = wide - rows
    mask = mask_by_column(lens_ref, slots_ref, rows, rank)
    normed = recv_ref[:, :, :share].reshape(rows, share)
    every = lax.dot_general(down_ref[...], normed, NT, preferred_element_type=F32) * mask
    slots = every.shape[0] // rank
    low = jnp.sum(every.reshape(slots, rank, rows), axis=0).astype(BF)
    back = jnp.sum(recv_ref[:, :, share:].astype(F32), axis=0).astype(BF).astype(F32)
    left = (mask.reshape(slots, rank, rows) * back[None]).reshape(slots * rank, rows).astype(BF)
    left_ref[...] = left
    term = SCALE * lax.dot_general(left, down_ref[...], TN, preferred_element_type=F32)
    send_ref[:, :, :share] = term.astype(BF).reshape(tp, own, share)
    for q in range(tp):
        send_ref[q, :, share:] = low


def down_kernel(left_ref, recv_ref, out_ref):
    tp, own, wide = recv_ref.shape
    rows = tp * own
    share = wide - rows
    normed = recv_ref[:, :, :share].reshape(rows, share)
    out_ref[...] = SCALE * jnp.dot(left_ref[...], normed, preferred_element_type=F32)


def up_kernel(rank, lens_ref, slots_ref, recv_ref, cot_ref, out_ref):
    tp, own, wide = recv_ref.shape
    rows = tp * own
    share = wide - rows
    mask = mask_by_column(lens_ref, slots_ref, rows, rank)
    slots = mask.shape[0] // rank
    low = jnp.sum(recv_ref[:, :, share:].astype(F32), axis=0).astype(BF).astype(F32)
    left = (mask.reshape(slots, rank, rows) * low[None]).reshape(slots * rank, rows).astype(BF)
    out_ref[...] = SCALE * lax.dot_general(cot_ref[...], left, NT, preferred_element_type=F32)


def final_kernel(pieces, recv_ref, tok_ref, *refs):
    out_ref = refs[-1]
    tp, own, _ = recv_ref.shape
    width = tok_ref.shape[1]
    share = width // tp
    chunks = []
    at = 0
    for n in pieces:
        total = refs[at][...].astype(F32)
        for r in refs[at + 1 : at + n]:
            total = total + r[...].astype(F32)
        at += n
        chunks.append(total)
    term = jnp.concatenate([recv_ref[q, :, :share].astype(F32) for q in range(tp)], axis=1)
    grad = jnp.concatenate(chunks, axis=1) + term
    tok = tok_ref[...].astype(F32)
    inv = lax.rsqrt(jnp.mean(tok * tok, axis=1, keepdims=True) + EPS)
    normed = tok * inv
    mean = jnp.mean(grad * normed, axis=1, keepdims=True)
    out_ref[...] = (inv * (grad - normed * mean)).astype(BF)


HBM = pl.BlockSpec(memory_space=pltpu.HBM)


def call(kernel, out, specs, scratch=(), flops=0, nbytes=0, vmem=48, out_specs=None, alias=None):
    return pl.pallas_call(
        kernel,
        out_shape=out,
        in_specs=specs,
        out_specs=jax.tree.map(lambda _: VMEM, out) if out_specs is None else out_specs,
        scratch_shapes=list(scratch),
        input_output_aliases=alias or {},
        cost_estimate=pl.CostEstimate(flops=int(flops), bytes_accessed=int(nbytes), transcendentals=0),
        compiler_params=pltpu.CompilerParams(vmem_limit_bytes=vmem << 20),
    )


def shape(dims, dtype=BF):
    return jax.ShapeDtypeStruct(dims, dtype)


def body(tokens, cotangent, weight, down_maps, up_maps, lengths, slots):
    tp = lax.axis_size("tp")
    me = lax.axis_index("tp").reshape(1)
    own, width = tokens.shape
    rows = own * tp
    count, rank, share = down_maps.shape
    columns = cotangent.shape[0]
    stages = stages_of(tp)
    order = block_order(stages)
    lens = lengths.reshape(1, count)
    slot = slots.reshape(1, count)
    down_flat = down_maps.reshape(count * rank, share)

    half = width // 2
    block = half // 4
    m = len(stages[0])
    each = rows // m
    dma = pltpu.SemaphoreType.DMA
    cotp, *parts_a = call(
        functools.partial(first_kernel, order, own, block),
        [shape((rows, columns))] + [shape((each, half))] * m,
        [SMEM, HBM, HBM],
        scratch=[
            pltpu.VMEM((columns, rows), BF),
            pltpu.VMEM((rows, columns), BF),
            pltpu.VMEM((columns, half), BF),
            dma,
            dma((half // block,)),
        ],
        flops=2 * rows * columns * half,
        nbytes=2 * columns * half,
    )(me, cotangent, weight)

    def pairs(m):
        return [(i, i ^ m) for i in range(tp)]

    def exchange(stage, parts):
        return [parts[0]] + [lax.ppermute(part, "tp", pairs(m)) for m, part in zip(stages[stage][1:], parts[1:])]

    def summed(groups, stage_of, passed=()):
        flat = [t for g in groups for t in g]
        cuts = [len(stages[s]) for s in stage_of]
        out = []
        for g, c in zip(groups, cuts):
            out += [shape((g[0].shape[0] // c, g[0].shape[1]))] * c
        n = len(flat)
        res = call(
            functools.partial(sum_kernel, [(len(g), c) for g, c in zip(groups, cuts)], len(passed)),
            out + [shape(x.shape, x.dtype) for x in passed],
            [VMEM] * n + [HBM] * len(passed),
            out_specs=[VMEM] * len(out) + [HBM] * len(passed),
            alias={n + i: len(out) + i for i in range(len(passed))},
            nbytes=4 * sum(x.size for x in flat),
        )(*flat, *passed)
        cut, at = [], 0
        for c in cuts:
            cut.append(list(res[at : at + c]))
            at += c
        return cut, list(res[at:])

    send, *parts_b = call(
        functools.partial(second_kernel, order, rank, half, block),
        [shape((tp, own, share + rows))] + [shape((each, half))] * m,
        [SMEM, VMEM, VMEM, VMEM, HBM, HBM, HBM],
        scratch=[
            pltpu.VMEM((own, width), BF),
            pltpu.VMEM((columns, count * rank), BF),
            pltpu.VMEM((columns, half), BF),
            pltpu.VMEM((rows, count * rank), F32),
            dma((2,)),
            dma((half // block,)),
        ],
        out_specs=[VMEM] * (1 + m),
        flops=2 * rows * columns * (half + count * rank),
        nbytes=2 * columns * (half + count * rank),
    )(me, lens, slot, cotp, tokens, up_maps, weight)

    last = len(stages) - 1
    held_a = exchange(0, parts_a)
    held_b = exchange(0, parts_b)
    (cut_a,), (send,) = summed([held_a], [1], [send])
    recv = lax.all_to_all(send, "tp", split_axis=0, concat_axis=0, tiled=True)
    for stage in range(1, last + 1):
        held_a = exchange(stage, cut_a)
        if stage < last:
            (cut_a, cut_b), _ = summed([held_a, held_b], [stage + 1, stage])
        else:
            (cut_b,), _ = summed([held_b], [stage])
        held_b = exchange(stage, cut_b)
    chunks = [held_a, held_b]

    send2, left = call(
        functools.partial(middle_kernel, rank),
        (shape((tp, own, share + rows)), shape((count * rank, rows))),
        [VMEM] * 4,
        flops=4 * rows * share * count * rank,
        nbytes=3 << 20,
    )(lens, slot, recv, down_flat)
    recv2 = lax.all_to_all(send2, "tp", split_axis=0, concat_axis=0, tiled=True)
    down_grad = call(
        down_kernel,
        shape((count * rank, share), F32),
        [VMEM] * 2,
        flops=2 * rows * share * count * rank,
        nbytes=3 << 20,
    )(left, recv)
    up_grad = call(
        functools.partial(up_kernel, rank),
        shape((columns, count * rank), F32),
        [VMEM] * 4,
        flops=2 * rows * columns * count * rank,
        nbytes=3 << 20,
    )(lens, slot, recv2, cotangent)
    flat = [piece for chunk in chunks for piece in chunk]
    grad_tokens = call(
        functools.partial(final_kernel, [len(c) for c in chunks]),
        shape((own, width)),
        [VMEM] * (2 + len(flat)),
        nbytes=2 << 20,
    )(recv2, tokens, *flat)
    return grad_tokens, down_grad.reshape(count, rank, share), up_grad


def solution(mesh):
    in_specs = (
        P(("rep", "tp"), None),
        P("tp", "rep"),
        P("tp", None),
        P(None, None, "tp"),
        P("tp", None),
        P("rep"),
        P(),
    )
    out_specs = (P(("rep", "tp"), None), P("rep", None, "tp"), P("tp", "rep"))
    return jax.shard_map(body, mesh=mesh, in_specs=in_specs, out_specs=out_specs, check_vma=False)
```

```python
import functools

import jax
import jax.numpy as jnp
from jax import lax
from jax.experimental import pallas as pl
from jax.experimental.pallas import tpu as pltpu
from jax.sharding import PartitionSpec as P

SCALE = 2.0
EPS = 1e-06
BF = jnp.bfloat16
F32 = jnp.float32
NT = (((1,), (1,)), ((), ()))
TN = (((0,), (0,)), ((), ()))
VMEM = pl.BlockSpec(memory_space=pltpu.VMEM)
SMEM = pl.BlockSpec(memory_space=pltpu.SMEM)


def stages_of(tp):
    bits = [1 << b for b in range(tp.bit_length() - 1)]
    groups = [bits[:1], bits[1:2]]
    rest = bits[2:]
    groups += [rest[i : i + 2] for i in range(0, len(rest), 2)]
    stages = []
    for group in groups:
        masks = [0]
        for b in group:
            masks = masks + [m | b for m in masks]
        if len(masks) > 1:
            stages.append(masks)
    return stages


def block_order(stages):
    order = [0]
    for masks in stages:
        order = [o | m for o in order for m in masks]
    return order


def iota(shape, dim):
    return lax.broadcasted_iota(jnp.int32, shape, dim)


def membership(lens_ref, slots_ref, rows):
    count = lens_ref.shape[1]
    lens = jnp.broadcast_to(lens_ref[...].astype(F32), (8, count)).astype(BF)
    upto = (iota((count, count), 0) <= iota((count, count), 1)).astype(F32).astype(BF)
    ends = jnp.dot(lens, upto, preferred_element_type=F32)[:1].astype(jnp.int32)
    starts = ends - lens_ref[...]
    position = iota((rows, count), 0)
    member = ((position >= starts) & (position < ends)).astype(F32).astype(BF)
    match = (iota((count, count), 0) == slots_ref[...]).astype(F32).astype(BF)
    return member, match


def mask_by_column(lens_ref, slots_ref, rows, rank):
    member, match = membership(lens_ref, slots_ref, rows)
    chosen = lax.dot_general(match, member, NT, preferred_element_type=F32).astype(BF)
    slots = match.shape[0]
    wide = (iota((slots * rank, slots), 0) // rank == iota((slots * rank, slots), 1)).astype(F32).astype(BF)
    return jnp.dot(wide, chosen, preferred_element_type=F32)


def cast_parts(out, parts):
    each = parts[0].shape[0]
    for i, part in enumerate(parts):
        part[...] = out[i * each : (i + 1) * each].astype(BF)


def fetch_weight(weight_hbm, wbuf, sems, first, block):
    copies = []
    for i in range(wbuf.shape[1] // block):
        copies.append(
            pltpu.make_async_copy(
                weight_hbm.at[:, pl.ds(first + i * block, block)], wbuf.at[:, pl.ds(i * block, block)], sems.at[i]
            )
        )
    return copies


def multiply(cotp, wbuf, copies, block, parts):
    each = parts[0].shape[0]
    for i, copy in enumerate(copies):
        copy.wait()
        columns = pl.ds(i * block, block)
        out = jnp.dot(cotp, wbuf[:, columns], preferred_element_type=F32)
        for k, part in enumerate(parts):
            part[:, columns] = out[k * each : (k + 1) * each].astype(BF)


def first_kernel(order, own, block, me_ref, cot_hbm, weight_hbm, cotp_ref, *refs):
    *parts, cot, cott, wbuf, sem, sems = refs
    cot_copy = pltpu.make_async_copy(cot_hbm, cot, sem)
    cot_copy.start()
    copies = fetch_weight(weight_hbm, wbuf, sems, 0, block)
    for copy in copies:
        copy.start()
    cot_copy.wait()
    cott[...] = cot[...].astype(F32).T.astype(BF)
    me = me_ref[0]
    for i, mask_bits in enumerate(order):
        source = pl.multiple_of((me ^ mask_bits) * own, own)
        cotp_ref[pl.ds(i * own, own), :] = cott[pl.ds(source, own), :]
    multiply(cotp_ref[...], wbuf, copies, block, parts)


def second_kernel(order, rank, first, block, me_ref, lens_ref, slots_ref, cotp_ref, tok_hbm, up_hbm, weight_hbm, send_hbm, *refs):
    *parts, send_ref, tokv, up, wbuf, back_rows, sem, sems = refs
    tp, own, _ = send_ref.shape
    width = tokv.shape[1]
    share = width // tp
    rows = cotp_ref.shape[0]
    tok_copy = pltpu.make_async_copy(tok_hbm, tokv, sem.at[0])
    tok_copy.start()
    up_copy = pltpu.make_async_copy(up_hbm, up, sem.at[1])
    up_copy.start()
    copies = fetch_weight(weight_hbm, wbuf, sems, first, block)
    for copy in copies:
        copy.start()
    member, match = membership(lens_ref, slots_ref, rows)
    chosen = lax.dot_general(member, match, NT, preferred_element_type=F32).astype(BF)
    slots = match.shape[0]
    wide = (iota((slots, slots * rank), 1) // rank == iota((slots, slots * rank), 0)).astype(F32).astype(BF)
    mask = jnp.dot(chosen, wide, preferred_element_type=F32)
    me = me_ref[0]
    tok_copy.wait()
    tok = tokv[...].astype(F32)
    inv = lax.rsqrt(jnp.mean(tok * tok, axis=1, keepdims=True) + EPS)
    normed = (tok * inv).astype(BF)
    up_copy.wait()
    every = jnp.dot(cotp_ref[...], up[...], preferred_element_type=F32)
    for i, mask_bits in enumerate(order):
        target = pl.multiple_of((me ^ mask_bits) * own, own)
        back_rows[pl.ds(target, own), :] = every[i * own : (i + 1) * own]
    every = back_rows[...] * mask
    lanes = every[:, :128]
    for i in range(1, slots * rank // 128):
        lanes = lanes + every[:, i * 128 : (i + 1) * 128]
    turned = lanes.T
    back = turned[:rank]
    for i in range(1, 128 // rank):
        back = back + turned[i * rank : (i + 1) * rank]
    back = back.astype(BF)
    for q in range(tp):
        send_ref[q, :, :share] = normed[:, q * share : (q + 1) * share]
        send_ref[q, :, share:] = back
    send_copy = pltpu.make_async_copy(send_ref, send_hbm, sem.at[2])
    send_copy.start()
    multiply(cotp_ref[...], wbuf, copies, block, parts)
    send_copy.wait()


def total_of(refs, i, each):
    total = refs[0][i * each : (i + 1) * each].astype(F32)
    for r in refs[1:]:
        total = total + r[i * each : (i + 1) * each].astype(F32)
    return total.astype(BF)


def sum_kernel(groups, passed, *refs):
    n_in = sum(t for t, _ in groups)
    terms, outs = refs[: n_in], refs[n_in + passed :]
    at, to = 0, 0
    for n, m in groups:
        each = terms[at].shape[0] // m
        for i in range(m):
            outs[to + i][...] = total_of(terms[at : at + n], i, each)
        at, to = at + n, to + m


def mask_kernel(rank, lens_ref, slots_ref, after_hbm, send_hbm, mask_ref, send_out):
    mask_ref[...] = mask_by_column(lens_ref, slots_ref, mask_ref.shape[1], rank).astype(BF)


def middle_kernel(rank, mask_ref, recv_ref, down_ref, after_hbm, send_hbm, left_ref, send_ref, sem):
    tp, own, wide = recv_ref.shape
    rows = tp * own
    share = wide - rows
    mask = mask_ref[...].astype(F32)
    normed = recv_ref[:, :, :share].reshape(rows, share)
    every = lax.dot_general(down_ref[...], normed, NT, preferred_element_type=F32) * mask
    slots = every.shape[0] // rank
    low = jnp.sum(every.reshape(slots, rank, rows), axis=0).astype(BF)
    back = jnp.sum(recv_ref[:, :, share:].astype(F32), axis=0).astype(BF).astype(F32)
    left = (mask.reshape(slots, rank, rows) * back[None]).reshape(slots * rank, rows).astype(BF)
    left_ref[...] = left
    term = SCALE * lax.dot_general(left, down_ref[...], TN, preferred_element_type=F32)
    send_ref[:, :, :share] = term.astype(BF).reshape(tp, own, share)
    for q in range(tp):
        send_ref[q, :, share:] = low
    copy = pltpu.make_async_copy(send_ref, send_hbm, sem)
    copy.start()
    copy.wait()


def down_kernel(left_ref, recv_ref, out_ref):
    tp, own, wide = recv_ref.shape
    rows = tp * own
    share = wide - rows
    normed = recv_ref[:, :, :share].reshape(rows, share)
    out_ref[...] = SCALE * jnp.dot(left_ref[...], normed, preferred_element_type=F32)


def up_kernel(rank, mask_ref, recv_ref, cot_ref, out_ref):
    tp, own, wide = recv_ref.shape
    rows = tp * own
    share = wide - rows
    mask = mask_ref[...].astype(F32)
    slots = mask.shape[0] // rank
    low = jnp.sum(recv_ref[:, :, share:].astype(F32), axis=0).astype(BF).astype(F32)
    left = (mask.reshape(slots, rank, rows) * low[None]).reshape(slots * rank, rows).astype(BF)
    out_ref[...] = SCALE * lax.dot_general(cot_ref[...], left, NT, preferred_element_type=F32)


def final_kernel(pieces, recv_ref, tok_ref, *refs):
    out_ref = refs[-1]
    tp, own, _ = recv_ref.shape
    width = tok_ref.shape[1]
    share = width // tp
    chunks = []
    at = 0
    for n in pieces:
        total = refs[at][...].astype(F32)
        for r in refs[at + 1 : at + n]:
            total = total + r[...].astype(F32)
        at += n
        chunks.append(total)
    term = jnp.concatenate([recv_ref[q, :, :share].astype(F32) for q in range(tp)], axis=1)
    grad = jnp.concatenate(chunks, axis=1) + term
    tok = tok_ref[...].astype(F32)
    inv = lax.rsqrt(jnp.mean(tok * tok, axis=1, keepdims=True) + EPS)
    normed = tok * inv
    mean = jnp.mean(grad * normed, axis=1, keepdims=True)
    out_ref[...] = (inv * (grad - normed * mean)).astype(BF)


HBM = pl.BlockSpec(memory_space=pltpu.HBM)


def call(kernel, out, specs, scratch=(), flops=0, nbytes=0, vmem=48, out_specs=None, alias=None):
    return pl.pallas_call(
        kernel,
        out_shape=out,
        in_specs=specs,
        out_specs=jax.tree.map(lambda _: VMEM, out) if out_specs is None else out_specs,
        scratch_shapes=list(scratch),
        input_output_aliases=alias or {},
        cost_estimate=pl.CostEstimate(flops=int(flops), bytes_accessed=int(nbytes), transcendentals=0),
        compiler_params=pltpu.CompilerParams(vmem_limit_bytes=vmem << 20),
    )


def shape(dims, dtype=BF):
    return jax.ShapeDtypeStruct(dims, dtype)


def body(tokens, cotangent, weight, down_maps, up_maps, lengths, slots):
    tp = lax.axis_size("tp")
    me = lax.axis_index("tp").reshape(1)
    own, width = tokens.shape
    rows = own * tp
    count, rank, share = down_maps.shape
    columns = cotangent.shape[0]
    stages = stages_of(tp)
    order = block_order(stages)
    lens = lengths.reshape(1, count)
    slot = slots.reshape(1, count)
    down_flat = down_maps.reshape(count * rank, share)

    half = width // 2
    block = half // 4
    m = len(stages[0])
    each = rows // m
    dma = pltpu.SemaphoreType.DMA
    cotp, *parts_a = call(
        functools.partial(first_kernel, order, own, block),
        [shape((rows, columns))] + [shape((each, half))] * m,
        [SMEM, HBM, HBM],
        scratch=[
            pltpu.VMEM((columns, rows), BF),
            pltpu.VMEM((rows, columns), BF),
            pltpu.VMEM((columns, half), BF),
            dma,
            dma((half // block,)),
        ],
        flops=2 * rows * columns * half,
        nbytes=2 * columns * half,
    )(me, cotangent, weight)

    def pairs(m):
        return [(i, i ^ m) for i in range(tp)]

    def exchange(stage, parts):
        return [parts[0]] + [lax.ppermute(part, "tp", pairs(m)) for m, part in zip(stages[stage][1:], parts[1:])]

    def summed(groups, stage_of, passed=()):
        flat = [t for g in groups for t in g]
        cuts = [len(stages[s]) for s in stage_of]
        out = []
        for g, c in zip(groups, cuts):
            out += [shape((g[0].shape[0] // c, g[0].shape[1]))] * c
        n = len(flat)
        res = call(
            functools.partial(sum_kernel, [(len(g), c) for g, c in zip(groups, cuts)], len(passed)),
            out + [shape(x.shape, x.dtype) for x in passed],
            [VMEM] * n + [HBM] * len(passed),
            out_specs=[VMEM] * len(out) + [HBM] * len(passed),
            alias={n + i: len(out) + i for i in range(len(passed))},
            nbytes=4 * sum(x.size for x in flat),
        )(*flat, *passed)
        cut, at = [], 0
        for c in cuts:
            cut.append(list(res[at : at + c]))
            at += c
        return cut, list(res[at:])

    send, *parts_b = call(
        functools.partial(second_kernel, order, rank, half, block),
        [shape((tp, own, share + rows))] + [shape((each, half))] * m,
        [SMEM, VMEM, VMEM, VMEM, HBM, HBM, HBM],
        scratch=[
            pltpu.VMEM((tp, own, share + rows), BF),
            pltpu.VMEM((own, width), BF),
            pltpu.VMEM((columns, count * rank), BF),
            pltpu.VMEM((columns, half), BF),
            pltpu.VMEM((rows, count * rank), F32),
            dma((3,)),
            dma((half // block,)),
        ],
        out_specs=[HBM] + [VMEM] * m,
        flops=2 * rows * columns * (half + count * rank),
        nbytes=2 * columns * (half + count * rank),
    )(me, lens, slot, cotp, tokens, up_maps, weight)

    last = len(stages) - 1
    held_a = exchange(0, parts_a)
    held_b = exchange(0, parts_b)
    (cut_a,), _ = summed([held_a], [1])
    mask, send = call(
        functools.partial(mask_kernel, rank),
        [shape((count * rank, rows)), shape(send.shape)],
        [VMEM, VMEM, HBM, HBM],
        out_specs=[VMEM, HBM],
        alias={3: 1},
        flops=2 * rows * count * count * rank,
    )(lens, slot, cut_a[0], send)
    recv = lax.all_to_all(send, "tp", split_axis=0, concat_axis=0, tiled=True)
    for stage in range(1, last + 1):
        held_a = exchange(stage, cut_a)
        if stage < last:
            (cut_a, cut_b), _ = summed([held_a, held_b], [stage + 1, stage])
        else:
            (cut_b,), _ = summed([held_b], [stage])
        if stage == 1:
            after = cut_b[0]
        held_b = exchange(stage, cut_b)
    chunks = [held_a, held_b]

    send2, left = call(
        functools.partial(middle_kernel, rank),
        (shape((tp, own, share + rows)), shape((count * rank, rows))),
        [VMEM] * 3 + [HBM],
        scratch=[pltpu.VMEM((tp, own, share + rows), BF), dma],
        out_specs=[HBM, VMEM],
        flops=4 * rows * share * count * rank,
        nbytes=3 << 20,
    )(mask, recv, down_flat, after)
    recv2 = lax.all_to_all(send2, "tp", split_axis=0, concat_axis=0, tiled=True)
    down_grad = call(
        down_kernel,
        shape((count * rank, share), F32),
        [VMEM] * 2,
        flops=2 * rows * share * count * rank,
        nbytes=3 << 20,
    )(left, recv)
    up_grad = call(
        functools.partial(up_kernel, rank),
        shape((columns, count * rank), F32),
        [VMEM] * 3,
        flops=2 * rows * columns * count * rank,
        nbytes=3 << 20,
    )(mask, recv2, cotangent)
    flat = [piece for chunk in chunks for piece in chunk]
    grad_tokens = call(
        functools.partial(final_kernel, [len(c) for c in chunks]),
        shape((own, width)),
        [VMEM] * (2 + len(flat)),
        nbytes=2 << 20,
    )(recv2, tokens, *flat)
    return grad_tokens, down_grad.reshape(count, rank, share), up_grad


def solution(mesh):
    in_specs = (
        P(("rep", "tp"), None),
        P("tp", "rep"),
        P("tp", None),
        P(None, None, "tp"),
        P("tp", None),
        P("rep"),
        P(),
    )
    out_specs = (P(("rep", "tp"), None), P("rep", None, "tp"), P("tp", "rep"))
    return jax.shard_map(body, mesh=mesh, in_specs=in_specs, out_specs=out_specs, check_vma=False)
```

```python
import functools

import jax
import jax.numpy as jnp
from jax import lax
from jax.experimental import pallas as pl
from jax.experimental.pallas import tpu as pltpu
from jax.sharding import PartitionSpec as P

SCALE = 2.0
EPS = 1e-06
BF = jnp.bfloat16
F32 = jnp.float32
NT = (((1,), (1,)), ((), ()))
TN = (((0,), (0,)), ((), ()))
VMEM = pl.BlockSpec(memory_space=pltpu.VMEM)
SMEM = pl.BlockSpec(memory_space=pltpu.SMEM)


def stages_of(tp):
    bits = [1 << b for b in range(tp.bit_length() - 1)]
    groups = [bits[:1], bits[1:2]]
    rest = bits[2:]
    groups += [rest[i : i + 2] for i in range(0, len(rest), 2)]
    stages = []
    for group in groups:
        masks = [0]
        for b in group:
            masks = masks + [m | b for m in masks]
        if len(masks) > 1:
            stages.append(masks)
    return stages


def block_order(stages):
    order = [0]
    for masks in stages:
        order = [o | m for o in order for m in masks]
    return order


def came_from(order):
    came = [0]
    for masks in stages_of(len(order)):
        came = [m | c for m in masks for c in came]
    return came


def iota(shape, dim):
    return lax.broadcasted_iota(jnp.int32, shape, dim)


def membership(lens_ref, slots_ref, rows):
    count = lens_ref.shape[1]
    lens = jnp.broadcast_to(lens_ref[...].astype(F32), (8, count)).astype(BF)
    upto = (iota((count, count), 0) <= iota((count, count), 1)).astype(F32).astype(BF)
    ends = jnp.dot(lens, upto, preferred_element_type=F32)[:1].astype(jnp.int32)
    starts = ends - lens_ref[...]
    position = iota((rows, count), 0)
    member = ((position >= starts) & (position < ends)).astype(F32).astype(BF)
    match = (iota((count, count), 0) == slots_ref[...]).astype(F32).astype(BF)
    return member, match


def mask_by_column(lens_ref, slots_ref, rows, rank):
    member, match = membership(lens_ref, slots_ref, rows)
    chosen = lax.dot_general(match, member, NT, preferred_element_type=F32).astype(BF)
    slots = match.shape[0]
    wide = (iota((slots * rank, slots), 0) // rank == iota((slots * rank, slots), 1)).astype(F32).astype(BF)
    return jnp.dot(wide, chosen, preferred_element_type=F32)


def cast_parts(out, parts):
    each = parts[0].shape[0]
    for i, part in enumerate(parts):
        part[...] = out[i * each : (i + 1) * each].astype(BF)


def fetch_weight(weight_hbm, wbuf, sems, first, block):
    copies = []
    for i in range(wbuf.shape[1] // block):
        copies.append(
            pltpu.make_async_copy(
                weight_hbm.at[:, pl.ds(first + i * block, block)], wbuf.at[:, pl.ds(i * block, block)], sems.at[i]
            )
        )
    return copies


def multiply(cotp, wbuf, copies, block, parts):
    each = parts[0].shape[0]
    for i, copy in enumerate(copies):
        copy.wait()
        columns = pl.ds(i * block, block)
        out = jnp.dot(cotp, wbuf[:, columns], preferred_element_type=F32)
        for k, part in enumerate(parts):
            part[:, columns] = out[k * each : (k + 1) * each].astype(BF)


def first_kernel(order, own, block, me_ref, cot_hbm, weight_hbm, cotp_ref, *refs):
    *parts, cot, cott, wbuf, sem, sems = refs
    cot_copy = pltpu.make_async_copy(cot_hbm, cot, sem)
    cot_copy.start()
    copies = fetch_weight(weight_hbm, wbuf, sems, 0, block)
    for copy in copies:
        copy.start()
    cot_copy.wait()
    cott[...] = cot[...].astype(F32).T.astype(BF)
    me = me_ref[0]
    for i, mask_bits in enumerate(order):
        source = pl.multiple_of((me ^ mask_bits) * own, own)
        cotp_ref[pl.ds(i * own, own), :] = cott[pl.ds(source, own), :]
    multiply(cotp_ref[...], wbuf, copies, block, parts)


def split_rows(x, share):
    high = x.astype(BF)
    low = (x - high.astype(F32)).astype(BF)
    lanes = jnp.concatenate([high, low], axis=1)
    return [lanes[:, i : i + share] for i in range(0, lanes.shape[1], share)]


def join_rows(ref, first, rank, tokens):
    share = ref.shape[1]
    pieces = [ref[first + i * rank : first + (i + 1) * rank].astype(F32) for i in range(2 * tokens // share)]
    lanes = jnp.concatenate(pieces, axis=1) if len(pieces) > 1 else pieces[0]
    return lanes[:, :tokens] + lanes[:, tokens:]


def put_rows(ref, first, x):
    for i, piece in enumerate(split_rows(x, ref.shape[1])):
        ref[first + i * piece.shape[0] : first + (i + 1) * piece.shape[0]] = piece


def adapter_kernel(order, rank, me_ref, lens_ref, slots_ref, cotp_ref, tok_ref, up_ref, mask_ref, sum_ref, keep_ref, send_ref, normed_ref, back_rows):
    own, width = tok_ref.shape
    tp = len(order)
    share = width // tp
    rows = cotp_ref.shape[0]
    me = me_ref[0]
    tok = tok_ref[...].astype(F32)
    inv = lax.rsqrt(jnp.mean(tok * tok, axis=1, keepdims=True) + EPS)
    normed_ref[...] = (tok * inv).astype(BF)
    half = len(order) // 2
    for i, mask_bits in enumerate(order):
        block = normed_ref[:, pl.ds(pl.multiple_of((me ^ mask_bits) * share, share), share)]
        if i < half:
            keep_ref[i * own : (i + 1) * own] = block
        else:
            send_ref[(i - half) * own : (i - half + 1) * own] = block
    member, match = membership(lens_ref, slots_ref, rows)
    slots = match.shape[0]
    chosen = lax.dot_general(match, member, NT, preferred_element_type=F32).astype(BF)
    tall = (iota((slots * rank, slots), 0) // rank == iota((slots * rank, slots), 1)).astype(F32).astype(BF)
    mask_ref[...] = jnp.dot(tall, chosen, preferred_element_type=F32).astype(BF)
    chosen = lax.dot_general(member, match, NT, preferred_element_type=F32).astype(BF)
    wide = (iota((slots, slots * rank), 1) // rank == iota((slots, slots * rank), 0)).astype(F32).astype(BF)
    mask = jnp.dot(chosen, wide, preferred_element_type=F32)
    every = jnp.dot(cotp_ref[...], up_ref[...], preferred_element_type=F32)
    for i, mask_bits in enumerate(order):
        target = pl.multiple_of((me ^ mask_bits) * own, own)
        back_rows[pl.ds(target, own), :] = every[i * own : (i + 1) * own]
    every = back_rows[...] * mask
    lanes = every[:, :128]
    for i in range(1, slots * rank // 128):
        lanes = lanes + every[:, i * 128 : (i + 1) * 128]
    turned = lanes.T
    back = turned[:rank]
    for i in range(1, 128 // rank):
        back = back + turned[i * rank : (i + 1) * rank]
    sum_ref[...] = back
    put_rows(send_ref, half * own, back)


def second_kernel(first, block, cotp_ref, weight_hbm, *refs):
    *parts, wbuf, sems = refs
    copies = fetch_weight(weight_hbm, wbuf, sems, first, block)
    for copy in copies:
        copy.start()
    multiply(cotp_ref[...], wbuf, copies, block, parts)


def turn_kernel(sources, cuts, sum_in, keep_in, *refs):
    n_in = len(refs) - 1 - cuts
    got, sum_out, outs = refs[:n_in], refs[n_in], refs[n_in + 1 :]
    rank, tokens = sum_in.shape
    rows = keep_in.shape[0]
    total = sum_in[...]
    for g in got:
        total = total + join_rows(g, rows, rank, tokens)
    sum_out[...] = total
    per = rows // sources
    each = per // cuts
    for c in range(cuts):
        at = 0
        for piece in (keep_in,) + tuple(got):
            for k in range(sources):
                outs[c][at : at + each] = piece[k * per + c * each : k * per + (c + 1) * each]
                at += each
        if c:
            put_rows(outs[c], at, total)


def total_of(refs, i, each):
    total = refs[0][i * each : (i + 1) * each].astype(F32)
    for r in refs[1:]:
        total = total + r[i * each : (i + 1) * each].astype(F32)
    return total.astype(BF)


def sum_kernel(groups, passed, *refs):
    n_in = sum(t for t, _ in groups)
    terms, outs = refs[: n_in], refs[n_in + passed :]
    at, to = 0, 0
    for n, m in groups:
        each = terms[at].shape[0] // m
        for i in range(m):
            outs[to + i][...] = total_of(terms[at : at + n], i, each)
        at, to = at + n, to + m


def middle_kernel(rank, order, me_ref, mask_ref, down_ref, sum_in, keep_in, *refs):
    *got, left_ref, normed_ref, sum_ref, keep_ref, send_ref, term_ref = refs
    rows, share = normed_ref.shape
    tp = len(order)
    own = rows // tp
    me = me_ref[0]
    per = keep_in.shape[0]
    back = sum_in[...]
    for g in got:
        back = back + join_rows(g, per, rank, rows)
    at = 0
    came = came_from(order)
    for piece in (keep_in,) + tuple(got):
        for k in range(per // own):
            target = pl.multiple_of((me ^ came[at]) * own, own)
            normed_ref[pl.ds(target, own), :] = piece[k * own : (k + 1) * own]
            at += 1
    mask = mask_ref[...].astype(F32)
    slots = mask.shape[0] // rank
    back = back.astype(BF).astype(F32)
    left = (mask.reshape(slots, rank, rows) * back[None]).reshape(slots * rank, rows).astype(BF)
    left_ref[...] = left
    every = lax.dot_general(down_ref[...], normed_ref[...], NT, preferred_element_type=F32) * mask
    low = jnp.sum(every.reshape(slots, rank, rows), axis=0)
    sum_ref[...] = low
    term_ref[...] = (SCALE * lax.dot_general(left, down_ref[...], TN, preferred_element_type=F32)).astype(BF)
    half = tp // 2
    for i, mask_bits in enumerate(order):
        block = term_ref[pl.ds(pl.multiple_of((me ^ mask_bits) * own, own), own), :]
        if i < half:
            keep_ref[i * own : (i + 1) * own] = block
        else:
            send_ref[(i - half) * own : (i - half + 1) * own] = block
    put_rows(send_ref, half * own, low)


def down_kernel(left_ref, normed_ref, out_ref):
    out_ref[...] = SCALE * jnp.dot(left_ref[...], normed_ref[...], preferred_element_type=F32)


def up_kernel(rank, rows_of_piece, mask_ref, cot_ref, sum_in, *refs):
    *got, out_ref = refs
    low = sum_in[...]
    for g in got:
        low = low + join_rows(g, rows_of_piece, rank, low.shape[1])
    low = low.astype(BF).astype(F32)
    mask = mask_ref[...].astype(F32)
    slots = mask.shape[0] // rank
    rows = mask.shape[1]
    left = (mask.reshape(slots, rank, rows) * low[None]).reshape(slots * rank, rows).astype(BF)
    out_ref[...] = SCALE * lax.dot_general(cot_ref[...], left, NT, preferred_element_type=F32)


def final_kernel(pieces, order, me_ref, tok_ref, keep_in, *refs):
    *refs, out_ref, term_ref = refs
    own, width = tok_ref.shape
    share = width // len(order)
    me = me_ref[0]
    n_got = len(refs) - sum(pieces)
    got, refs = refs[:n_got], refs[n_got:]
    came = came_from(order)
    at = 0
    for piece in (keep_in,) + tuple(got):
        for k in range(keep_in.shape[0] // own):
            target = pl.multiple_of((me ^ came[at]) * share, share)
            term_ref[:, pl.ds(target, share)] = piece[k * own : (k + 1) * own].astype(F32)
            at += 1
    chunks = []
    at = 0
    for n in pieces:
        total = refs[at][...].astype(F32)
        for r in refs[at + 1 : at + n]:
            total = total + r[...].astype(F32)
        at += n
        chunks.append(total)
    grad = jnp.concatenate(chunks, axis=1) + term_ref[...]
    tok = tok_ref[...].astype(F32)
    inv = lax.rsqrt(jnp.mean(tok * tok, axis=1, keepdims=True) + EPS)
    normed = tok * inv
    mean = jnp.mean(grad * normed, axis=1, keepdims=True)
    out_ref[...] = (inv * (grad - normed * mean)).astype(BF)


HBM = pl.BlockSpec(memory_space=pltpu.HBM)


def call(kernel, out, specs, scratch=(), flops=0, nbytes=0, vmem=48, out_specs=None, alias=None):
    return pl.pallas_call(
        kernel,
        out_shape=out,
        in_specs=specs,
        out_specs=jax.tree.map(lambda _: VMEM, out) if out_specs is None else out_specs,
        scratch_shapes=list(scratch),
        input_output_aliases=alias or {},
        cost_estimate=pl.CostEstimate(flops=int(flops), bytes_accessed=int(nbytes), transcendentals=0),
        compiler_params=pltpu.CompilerParams(vmem_limit_bytes=vmem << 20),
    )


def shape(dims, dtype=BF):
    return jax.ShapeDtypeStruct(dims, dtype)


def body(tokens, cotangent, weight, down_maps, up_maps, lengths, slots):
    tp = lax.axis_size("tp")
    me = lax.axis_index("tp").reshape(1)
    own, width = tokens.shape
    rows = own * tp
    count, rank, share = down_maps.shape
    columns = cotangent.shape[0]
    stages = stages_of(tp)
    order = block_order(stages)
    lens = lengths.reshape(1, count)
    slot = slots.reshape(1, count)
    down_flat = down_maps.reshape(count * rank, share)

    half = width // 2
    block = half // 4
    m = len(stages[0])
    each = rows // m
    dma = pltpu.SemaphoreType.DMA
    cotp, *parts_a = call(
        functools.partial(first_kernel, order, own, block),
        [shape((rows, columns))] + [shape((each, half))] * m,
        [SMEM, HBM, HBM],
        scratch=[
            pltpu.VMEM((columns, rows), BF),
            pltpu.VMEM((rows, columns), BF),
            pltpu.VMEM((columns, half), BF),
            dma,
            dma((half // block,)),
        ],
        flops=2 * rows * columns * half,
        nbytes=2 * columns * half,
    )(me, cotangent, weight)

    def pairs(m):
        return [(i, i ^ m) for i in range(tp)]

    def exchange(stage, parts):
        return [parts[0]] + [lax.ppermute(part, "tp", pairs(m)) for m, part in zip(stages[stage][1:], parts[1:])]

    def summed(groups, stage_of, passed=()):
        flat = [t for g in groups for t in g]
        cuts = [len(stages[s]) for s in stage_of]
        out = []
        for g, c in zip(groups, cuts):
            out += [shape((g[0].shape[0] // c, g[0].shape[1]))] * c
        n = len(flat)
        res = call(
            functools.partial(sum_kernel, [(len(g), c) for g, c in zip(groups, cuts)], len(passed)),
            out + [shape(x.shape, x.dtype) for x in passed],
            [VMEM] * n + [HBM] * len(passed),
            out_specs=[VMEM] * len(out) + [HBM] * len(passed),
            alias={n + i: len(out) + i for i in range(len(passed))},
            nbytes=4 * sum(x.size for x in flat),
        )(*flat, *passed)
        cut, at = [], 0
        for c in cuts:
            cut.append(list(res[at : at + c]))
            at += c
        return cut, list(res[at:])

    extra = 2 * rows * rank // share
    mask, partial, keep, gift = call(
        functools.partial(adapter_kernel, order, rank),
        [
            shape((count * rank, rows)),
            shape((rank, rows), F32),
            shape((rows // 2, share)),
            shape((rows // 2 + extra, share)),
        ],
        [SMEM, VMEM, VMEM, VMEM, VMEM, VMEM],
        scratch=[pltpu.VMEM((own, width), BF), pltpu.VMEM((rows, count * rank), F32)],
        flops=2 * rows * columns * count * rank,
        nbytes=2 * columns * count * rank,
    )(me, lens, slot, cotp, tokens, up_maps)
    *parts_b, = call(
        functools.partial(second_kernel, half, block),
        [shape((each, half))] * m,
        [VMEM, HBM],
        scratch=[pltpu.VMEM((columns, half), BF), dma((half // block,))],
        flops=2 * rows * columns * half,
        nbytes=2 * columns * half,
    )(cotp, weight)

    def shuffled(partial, keep, gift):
        parts = [gift]
        for stage in range(len(stages)):
            got = [lax.ppermute(g, "tp", pairs(k)) for k, g in zip(stages[stage][1:], parts)]
            if stage == len(stages) - 1:
                return partial, keep, got
            sources = 1
            for masks in stages[:stage]:
                sources *= len(masks)
            cuts = len(stages[stage + 1])
            size = keep.shape[0] * len(stages[stage]) // cuts
            partial, keep, *parts = call(
                functools.partial(turn_kernel, sources, cuts),
                [shape((rank, rows), F32), shape((size, share))] + [shape((size + extra, share))] * (cuts - 1),
                [VMEM] * (2 + len(got)),
                nbytes=4 * keep.size * 4,
            )(partial, keep, *got)

    last = len(stages) - 1
    held_a = exchange(0, parts_a)
    partial, keep, got = shuffled(partial, keep, gift)
    held_b = exchange(0, parts_b)
    (cut_a,), _ = summed([held_a], [1])
    for stage in range(1, last + 1):
        held_a = exchange(stage, cut_a)
        if stage < last:
            (cut_a, cut_b), _ = summed([held_a, held_b], [stage + 1, stage])
        else:
            (cut_b,), _ = summed([held_b], [stage])
        held_b = exchange(stage, cut_b)
    chunks = [held_a, held_b]

    left, normed, partial, keep, gift = call(
        functools.partial(middle_kernel, rank, order),
        [
            shape((count * rank, rows)),
            shape((rows, share)),
            shape((rank, rows), F32),
            shape((rows // 2, share)),
            shape((rows // 2 + extra, share)),
        ],
        [SMEM] + [VMEM] * (4 + len(got)),
        scratch=[pltpu.VMEM((rows, share), BF)],
        flops=4 * rows * share * count * rank,
        nbytes=3 << 20,
    )(me, mask, down_flat, partial, keep, *got)
    down_grad = call(
        down_kernel,
        shape((count * rank, share), F32),
        [VMEM] * 2,
        flops=2 * rows * share * count * rank,
        nbytes=3 << 20,
    )(left, normed)
    partial, keep, got = shuffled(partial, keep, gift)
    up_grad = call(
        functools.partial(up_kernel, rank, keep.shape[0]),
        shape((columns, count * rank), F32),
        [VMEM] * (3 + len(got)),
        flops=2 * rows * columns * count * rank,
        nbytes=3 << 20,
    )(mask, cotangent, partial, *got)
    flat = [piece for chunk in chunks for piece in chunk]
    grad_tokens = call(
        functools.partial(final_kernel, [len(c) for c in chunks], order),
        shape((own, width)),
        [SMEM] + [VMEM] * (2 + len(got) + len(flat)),
        scratch=[pltpu.VMEM((own, width), F32)],
        nbytes=2 << 20,
    )(me, tokens, keep, *got, *flat)
    return grad_tokens, down_grad.reshape(count, rank, share), up_grad


def solution(mesh):
    in_specs = (
        P(("rep", "tp"), None),
        P("tp", "rep"),
        P("tp", None),
        P(None, None, "tp"),
        P("tp", None),
        P("rep"),
        P(),
    )
    out_specs = (P(("rep", "tp"), None), P("rep", None, "tp"), P("tp", "rep"))
    return jax.shard_map(body, mesh=mesh, in_specs=in_specs, out_specs=out_specs, check_vma=False)
```

```python
import functools

import jax
import jax.numpy as jnp
from jax import lax
from jax.experimental import pallas as pl
from jax.experimental.pallas import tpu as pltpu
from jax.sharding import PartitionSpec as P

SCALE = 2.0
EPS = 1e-06
BF = jnp.bfloat16
F32 = jnp.float32
NT = (((1,), (1,)), ((), ()))
TN = (((0,), (0,)), ((), ()))
VMEM = pl.BlockSpec(memory_space=pltpu.VMEM)
SMEM = pl.BlockSpec(memory_space=pltpu.SMEM)


def stages_of(tp):
    bits = [1 << b for b in range(tp.bit_length() - 1)]
    groups = [bits[:1], bits[1:2]]
    rest = bits[2:]
    groups += [rest[i : i + 2] for i in range(0, len(rest), 2)]
    stages = []
    for group in groups:
        masks = [0]
        for b in group:
            masks = masks + [m | b for m in masks]
        if len(masks) > 1:
            stages.append(masks)
    return stages


def block_order(stages):
    order = [0]
    for masks in stages:
        order = [o | m for o in order for m in masks]
    return order


def iota(shape, dim):
    return lax.broadcasted_iota(jnp.int32, shape, dim)


def membership(lens_ref, slots_ref, rows):
    count = lens_ref.shape[1]
    lens = jnp.broadcast_to(lens_ref[...].astype(F32), (8, count)).astype(BF)
    upto = (iota((count, count), 0) <= iota((count, count), 1)).astype(F32).astype(BF)
    ends = jnp.dot(lens, upto, preferred_element_type=F32)[:1].astype(jnp.int32)
    starts = ends - lens_ref[...]
    position = iota((rows, count), 0)
    member = ((position >= starts) & (position < ends)).astype(F32).astype(BF)
    match = (iota((count, count), 0) == slots_ref[...]).astype(F32).astype(BF)
    return member, match


def mask_by_column(lens_ref, slots_ref, rows, rank):
    member, match = membership(lens_ref, slots_ref, rows)
    chosen = lax.dot_general(match, member, NT, preferred_element_type=F32).astype(BF)
    slots = match.shape[0]
    wide = (iota((slots * rank, slots), 0) // rank == iota((slots * rank, slots), 1)).astype(F32).astype(BF)
    return jnp.dot(wide, chosen, preferred_element_type=F32)


def cast_parts(out, parts):
    each = parts[0].shape[0]
    for i, part in enumerate(parts):
        part[...] = out[i * each : (i + 1) * each].astype(BF)


def fetch_weight(weight_hbm, wbuf, sems, first, block):
    copies = []
    for i in range(wbuf.shape[1] // block):
        copies.append(
            pltpu.make_async_copy(
                weight_hbm.at[:, pl.ds(first + i * block, block)], wbuf.at[:, pl.ds(i * block, block)], sems.at[i]
            )
        )
    return copies


def multiply(cotp, wbuf, copies, block, parts):
    each = parts[0].shape[0]
    for i, copy in enumerate(copies):
        copy.wait()
        columns = pl.ds(i * block, block)
        out = jnp.dot(cotp, wbuf[:, columns], preferred_element_type=F32)
        for k, part in enumerate(parts):
            part[:, columns] = out[k * each : (k + 1) * each].astype(BF)


def first_kernel(order, own, block, me_ref, cot_hbm, weight_hbm, cotp_ref, *refs):
    *parts, cot, cott, wbuf, sem, sems = refs
    cot_copy = pltpu.make_async_copy(cot_hbm, cot, sem)
    cot_copy.start()
    copies = fetch_weight(weight_hbm, wbuf, sems, 0, block)
    for copy in copies:
        copy.start()
    cot_copy.wait()
    cott[...] = cot[...].astype(F32).T.astype(BF)
    me = me_ref[0]
    for i, mask_bits in enumerate(order):
        source = pl.multiple_of((me ^ mask_bits) * own, own)
        cotp_ref[pl.ds(i * own, own), :] = cott[pl.ds(source, own), :]
    multiply(cotp_ref[...], wbuf, copies, block, parts)


def second_kernel(order, rank, first, block, me_ref, lens_ref, slots_ref, cotp_ref, tok_hbm, up_hbm, weight_hbm, send_hbm, *refs):
    *parts, send_ref, tokv, up, wbuf, back_rows, sem, sems = refs
    tp, own, _ = send_ref.shape
    width = tokv.shape[1]
    share = width // tp
    rows = cotp_ref.shape[0]
    tok_copy = pltpu.make_async_copy(tok_hbm, tokv, sem.at[0])
    tok_copy.start()
    up_copy = pltpu.make_async_copy(up_hbm, up, sem.at[1])
    up_copy.start()
    copies = fetch_weight(weight_hbm, wbuf, sems, first, block)
    for copy in copies:
        copy.start()
    member, match = membership(lens_ref, slots_ref, rows)
    chosen = lax.dot_general(member, match, NT, preferred_element_type=F32).astype(BF)
    slots = match.shape[0]
    wide = (iota((slots, slots * rank), 1) // rank == iota((slots, slots * rank), 0)).astype(F32).astype(BF)
    mask = jnp.dot(chosen, wide, preferred_element_type=F32)
    me = me_ref[0]
    tok_copy.wait()
    tok = tokv[...].astype(F32)
    inv = lax.rsqrt(jnp.mean(tok * tok, axis=1, keepdims=True) + EPS)
    normed = (tok * inv).astype(BF)
    up_copy.wait()
    every = jnp.dot(cotp_ref[...], up[...], preferred_element_type=F32)
    for i, mask_bits in enumerate(order):
        target = pl.multiple_of((me ^ mask_bits) * own, own)
        back_rows[pl.ds(target, own), :] = every[i * own : (i + 1) * own]
    every = back_rows[...] * mask
    lanes = every[:, :128]
    for i in range(1, slots * rank // 128):
        lanes = lanes + every[:, i * 128 : (i + 1) * 128]
    turned = lanes.T
    back = turned[:rank]
    for i in range(1, 128 // rank):
        back = back + turned[i * rank : (i + 1) * rank]
    back = back.astype(BF)
    for q in range(tp):
        send_ref[q, :, :share] = normed[:, q * share : (q + 1) * share]
        send_ref[q, :, share:] = back
    send_copy = pltpu.make_async_copy(send_ref, send_hbm, sem.at[2])
    send_copy.start()
    multiply(cotp_ref[...], wbuf, copies, block, parts)
    send_copy.wait()


def total_of(refs, i, each):
    total = refs[0][i * each : (i + 1) * each].astype(F32)
    for r in refs[1:]:
        total = total + r[i * each : (i + 1) * each].astype(F32)
    return total.astype(BF)


def sum_kernel(groups, passed, *refs):
    n_in = sum(t for t, _ in groups)
    terms, outs = refs[: n_in], refs[n_in + passed :]
    at, to = 0, 0
    for n, m in groups:
        each = terms[at].shape[0] // m
        for i in range(m):
            outs[to + i][...] = total_of(terms[at : at + n], i, each)
        at, to = at + n, to + m


def mask_kernel(rank, lens_ref, slots_ref, mask_ref):
    mask_ref[...] = mask_by_column(lens_ref, slots_ref, mask_ref.shape[1], rank).astype(BF)


def middle_kernel(rank, mask_ref, recv_ref, down_ref, send_hbm, left_ref, send_ref, sem):
    tp, own, wide = recv_ref.shape
    rows = tp * own
    share = wide - rows
    mask = mask_ref[...].astype(F32)
    normed = recv_ref[:, :, :share].reshape(rows, share)
    every = lax.dot_general(down_ref[...], normed, NT, preferred_element_type=F32) * mask
    slots = every.shape[0] // rank
    low = jnp.sum(every.reshape(slots, rank, rows), axis=0).astype(BF)
    back = jnp.sum(recv_ref[:, :, share:].astype(F32), axis=0).astype(BF).astype(F32)
    left = (mask.reshape(slots, rank, rows) * back[None]).reshape(slots * rank, rows).astype(BF)
    left_ref[...] = left
    term = SCALE * lax.dot_general(left, down_ref[...], TN, preferred_element_type=F32)
    send_ref[:, :, :share] = term.astype(BF).reshape(tp, own, share)
    for q in range(tp):
        send_ref[q, :, share:] = low
    copy = pltpu.make_async_copy(send_ref, send_hbm, sem)
    copy.start()
    copy.wait()


def down_kernel(left_ref, recv_ref, out_ref):
    tp, own, wide = recv_ref.shape
    rows = tp * own
    share = wide - rows
    normed = recv_ref[:, :, :share].reshape(rows, share)
    out_ref[...] = SCALE * jnp.dot(left_ref[...], normed, preferred_element_type=F32)


def up_kernel(rank, mask_ref, recv_ref, cot_ref, out_ref):
    tp, own, wide = recv_ref.shape
    rows = tp * own
    share = wide - rows
    mask = mask_ref[...].astype(F32)
    slots = mask.shape[0] // rank
    low = jnp.sum(recv_ref[:, :, share:].astype(F32), axis=0).astype(BF).astype(F32)
    left = (mask.reshape(slots, rank, rows) * low[None]).reshape(slots * rank, rows).astype(BF)
    out_ref[...] = SCALE * lax.dot_general(cot_ref[...], left, NT, preferred_element_type=F32)


def final_kernel(pieces, recv_ref, tok_ref, *refs):
    out_ref = refs[-1]
    tp, own, _ = recv_ref.shape
    width = tok_ref.shape[1]
    share = width // tp
    chunks = []
    at = 0
    for n in pieces:
        total = refs[at][...].astype(F32)
        for r in refs[at + 1 : at + n]:
            total = total + r[...].astype(F32)
        at += n
        chunks.append(total)
    term = jnp.concatenate([recv_ref[q, :, :share].astype(F32) for q in range(tp)], axis=1)
    grad = jnp.concatenate(chunks, axis=1) + term
    tok = tok_ref[...].astype(F32)
    inv = lax.rsqrt(jnp.mean(tok * tok, axis=1, keepdims=True) + EPS)
    normed = tok * inv
    mean = jnp.mean(grad * normed, axis=1, keepdims=True)
    out_ref[...] = (inv * (grad - normed * mean)).astype(BF)


HBM = pl.BlockSpec(memory_space=pltpu.HBM)


def call(kernel, out, specs, scratch=(), flops=0, nbytes=0, vmem=20, out_specs=None, alias=None):
    return pl.pallas_call(
        kernel,
        out_shape=out,
        in_specs=specs,
        out_specs=jax.tree.map(lambda _: VMEM, out) if out_specs is None else out_specs,
        scratch_shapes=list(scratch),
        input_output_aliases=alias or {},
        cost_estimate=pl.CostEstimate(flops=int(flops), bytes_accessed=int(nbytes), transcendentals=0),
        compiler_params=pltpu.CompilerParams(vmem_limit_bytes=vmem << 20),
    )


def shape(dims, dtype=BF):
    return jax.ShapeDtypeStruct(dims, dtype)


def body(tokens, cotangent, weight, down_maps, up_maps, lengths, slots):
    tp = lax.axis_size("tp")
    me = lax.axis_index("tp").reshape(1)
    own, width = tokens.shape
    rows = own * tp
    count, rank, share = down_maps.shape
    columns = cotangent.shape[0]
    stages = stages_of(tp)
    order = block_order(stages)
    lens = lengths.reshape(1, count)
    slot = slots.reshape(1, count)
    down_flat = down_maps.reshape(count * rank, share)

    half = width * 5 // 8
    block = 1024
    m = len(stages[0])
    each = rows // m
    dma = pltpu.SemaphoreType.DMA
    cotp, *parts_a = call(
        functools.partial(first_kernel, order, own, block),
        [shape((rows, columns))] + [shape((each, half))] * m,
        [SMEM, HBM, HBM],
        scratch=[
            pltpu.VMEM((columns, rows), BF),
            pltpu.VMEM((rows, columns), BF),
            pltpu.VMEM((columns, half), BF),
            dma,
            dma((half // block,)),
        ],
        vmem=48,
        flops=2 * rows * columns * half,
        nbytes=2 * columns * half,
    )(me, cotangent, weight)

    def pairs(m):
        return [(i, i ^ m) for i in range(tp)]

    def exchange(stage, parts):
        return [parts[0]] + [lax.ppermute(part, "tp", pairs(m)) for m, part in zip(stages[stage][1:], parts[1:])]

    def summed(groups, stage_of, passed=()):
        flat = [t for g in groups for t in g]
        cuts = [len(stages[s]) for s in stage_of]
        out = []
        for g, c in zip(groups, cuts):
            out += [shape((g[0].shape[0] // c, g[0].shape[1]))] * c
        n = len(flat)
        res = call(
            functools.partial(sum_kernel, [(len(g), c) for g, c in zip(groups, cuts)], len(passed)),
            out + [shape(x.shape, x.dtype) for x in passed],
            [VMEM] * n + [HBM] * len(passed),
            out_specs=[VMEM] * len(out) + [HBM] * len(passed),
            alias={n + i: len(out) + i for i in range(len(passed))},
            nbytes=4 * sum(x.size for x in flat),
        )(*flat, *passed)
        cut, at = [], 0
        for c in cuts:
            cut.append(list(res[at : at + c]))
            at += c
        return cut, list(res[at:])

    send, *parts_b = call(
        functools.partial(second_kernel, order, rank, half, block),
        [shape((tp, own, share + rows))] + [shape((each, width - half))] * m,
        [SMEM, VMEM, VMEM, VMEM, HBM, HBM, HBM],
        scratch=[
            pltpu.VMEM((tp, own, share + rows), BF),
            pltpu.VMEM((own, width), BF),
            pltpu.VMEM((columns, count * rank), BF),
            pltpu.VMEM((columns, width - half), BF),
            pltpu.VMEM((rows, count * rank), F32),
            dma((3,)),
            dma(((width - half) // block,)),
        ],
        out_specs=[HBM] + [VMEM] * m,
        vmem=48,
        flops=2 * rows * columns * (half + count * rank),
        nbytes=2 * columns * (half + count * rank),
    )(me, lens, slot, cotp, tokens, up_maps, weight)

    last = len(stages) - 1
    held_a = exchange(0, parts_a)
    held_b = exchange(0, parts_b)
    (cut_a,), _ = summed([held_a], [1])
    (mask,) = call(functools.partial(mask_kernel, rank), [shape((count * rank, rows))], [VMEM, VMEM])(lens, slot)
    recv = lax.all_to_all(send, "tp", split_axis=0, concat_axis=0, tiled=True)
    for stage in range(1, last + 1):
        held_a = exchange(stage, cut_a)
        if stage < last:
            (cut_a, cut_b), _ = summed([held_a, held_b], [stage + 1, stage])
        else:
            (cut_b,), _ = summed([held_b], [stage])
        held_b = exchange(stage, cut_b)
    chunks = [held_a, held_b]

    send2, left = call(
        functools.partial(middle_kernel, rank),
        (shape((tp, own, share + rows)), shape((count * rank, rows))),
        [VMEM] * 3,
        scratch=[pltpu.VMEM((tp, own, share + rows), BF), dma],
        out_specs=[HBM, VMEM],
        flops=4 * rows * share * count * rank,
        nbytes=3 << 20,
    )(mask, recv, down_flat)
    recv2 = lax.all_to_all(send2, "tp", split_axis=0, concat_axis=0, tiled=True)
    down_grad = call(
        down_kernel,
        shape((count * rank, share), F32),
        [VMEM] * 2,
        flops=2 * rows * share * count * rank,
        nbytes=3 << 20,
    )(left, recv)
    up_grad = call(
        functools.partial(up_kernel, rank),
        shape((columns, count * rank), F32),
        [VMEM] * 3,
        flops=2 * rows * columns * count * rank,
        nbytes=3 << 20,
    )(mask, recv2, cotangent)
    flat = [piece for chunk in chunks for piece in chunk]
    grad_tokens = call(
        functools.partial(final_kernel, [len(c) for c in chunks]),
        shape((own, width)),
        [VMEM] * (2 + len(flat)),
        nbytes=2 << 20,
    )(recv2, tokens, *flat)
    return grad_tokens, down_grad.reshape(count, rank, share), up_grad


def solution(mesh):
    in_specs = (
        P(("rep", "tp"), None),
        P("tp", "rep"),
        P("tp", None),
        P(None, None, "tp"),
        P("tp", None),
        P("rep"),
        P(),
    )
    out_specs = (P(("rep", "tp"), None), P("rep", None, "tp"), P("tp", "rep"))
    return jax.shard_map(body, mesh=mesh, in_specs=in_specs, out_specs=out_specs, check_vma=False)
```

```python
import functools

import jax
import jax.numpy as jnp
from jax import lax
from jax.experimental import pallas as pl
from jax.experimental.pallas import tpu as pltpu
from jax.sharding import PartitionSpec as P

SCALE = 2.0
EPS = 1e-06
BF = jnp.bfloat16
F32 = jnp.float32
NT = (((1,), (1,)), ((), ()))
TN = (((0,), (0,)), ((), ()))
VMEM = pl.BlockSpec(memory_space=pltpu.VMEM)
SMEM = pl.BlockSpec(memory_space=pltpu.SMEM)


def stages_of(tp):
    bits = [1 << b for b in range(tp.bit_length() - 1)]
    groups = [bits[:1], bits[1:2]]
    rest = bits[2:]
    groups += [rest[i : i + 2] for i in range(0, len(rest), 2)]
    stages = []
    for group in groups:
        masks = [0]
        for b in group:
            masks = masks + [m | b for m in masks]
        if len(masks) > 1:
            stages.append(masks)
    return stages


def block_order(stages):
    order = [0]
    for masks in stages:
        order = [o | m for o in order for m in masks]
    return order


def iota(shape, dim):
    return lax.broadcasted_iota(jnp.int32, shape, dim)


def membership(lens_ref, slots_ref, rows):
    count = lens_ref.shape[1]
    lens = jnp.broadcast_to(lens_ref[...].astype(F32), (8, count)).astype(BF)
    upto = (iota((count, count), 0) <= iota((count, count), 1)).astype(F32).astype(BF)
    ends = jnp.dot(lens, upto, preferred_element_type=F32)[:1].astype(jnp.int32)
    starts = ends - lens_ref[...]
    position = iota((rows, count), 0)
    member = ((position >= starts) & (position < ends)).astype(F32).astype(BF)
    match = (iota((count, count), 0) == slots_ref[...]).astype(F32).astype(BF)
    return member, match


def mask_by_column(lens_ref, slots_ref, rows, rank):
    member, match = membership(lens_ref, slots_ref, rows)
    chosen = lax.dot_general(match, member, NT, preferred_element_type=F32).astype(BF)
    slots = match.shape[0]
    wide = (iota((slots * rank, slots), 0) // rank == iota((slots * rank, slots), 1)).astype(F32).astype(BF)
    return jnp.dot(wide, chosen, preferred_element_type=F32)


def cast_parts(out, parts):
    each = parts[0].shape[0]
    for i, part in enumerate(parts):
        part[...] = out[i * each : (i + 1) * each].astype(BF)


def fetch_weight(weight_hbm, wbuf, sems, first, block):
    copies = []
    for i in range(wbuf.shape[1] // block):
        copies.append(
            pltpu.make_async_copy(
                weight_hbm.at[:, pl.ds(first + i * block, block)], wbuf.at[:, pl.ds(i * block, block)], sems.at[i]
            )
        )
    return copies


def multiply(cotp, wbuf, copies, block, parts):
    for i, copy in enumerate(copies):
        copy.wait()
        columns = pl.ds(i * block, block)
        out = jnp.dot(cotp, wbuf[:, columns], preferred_element_type=F32)
        at = 0
        for part in parts:
            part[:, columns] = out[at : at + part.shape[0]].astype(BF)
            at += part.shape[0]


def first_kernel(order, own, block, me_ref, cot_hbm, weight_hbm, cotp_ref, *refs):
    *parts, cot, cott, wbuf, sem, sems = refs
    cot_copy = pltpu.make_async_copy(cot_hbm, cot, sem)
    cot_copy.start()
    copies = fetch_weight(weight_hbm, wbuf, sems, 0, block)
    for copy in copies:
        copy.start()
    cot_copy.wait()
    cott[...] = cot[...].astype(F32).T.astype(BF)
    me = me_ref[0]
    for i, mask_bits in enumerate(order):
        source = pl.multiple_of((me ^ mask_bits) * own, own)
        cotp_ref[pl.ds(i * own, own), :] = cott[pl.ds(source, own), :]
    multiply(cotp_ref[...], wbuf, copies, block, parts)


def second_kernel(first, block, cotp_ref, after_hbm, weight_hbm, *refs):
    *parts, wbuf, sems = refs
    copies = fetch_weight(weight_hbm, wbuf, sems, first, block)
    for copy in copies:
        copy.start()
    multiply(cotp_ref[...], wbuf, copies, block, parts)


def adapter_kernel(order, rank, me_ref, lens_ref, slots_ref, cotp_ref, tok_hbm, up_hbm, send_hbm, send_ref, tokv, up, back_rows, sem):
    tp, own, _ = send_ref.shape
    width = tokv.shape[1]
    share = width // tp
    rows = cotp_ref.shape[0]
    tok_copy = pltpu.make_async_copy(tok_hbm, tokv, sem.at[0])
    tok_copy.start()
    up_copy = pltpu.make_async_copy(up_hbm, up, sem.at[1])
    up_copy.start()
    member, match = membership(lens_ref, slots_ref, rows)
    chosen = lax.dot_general(member, match, NT, preferred_element_type=F32).astype(BF)
    slots = match.shape[0]
    wide = (iota((slots, slots * rank), 1) // rank == iota((slots, slots * rank), 0)).astype(F32).astype(BF)
    mask = jnp.dot(chosen, wide, preferred_element_type=F32)
    me = me_ref[0]
    tok_copy.wait()
    tok = tokv[...].astype(F32)
    inv = lax.rsqrt(jnp.mean(tok * tok, axis=1, keepdims=True) + EPS)
    normed = (tok * inv).astype(BF)
    up_copy.wait()
    every = jnp.dot(cotp_ref[...], up[...], preferred_element_type=F32)
    for i, mask_bits in enumerate(order):
        target = pl.multiple_of((me ^ mask_bits) * own, own)
        back_rows[pl.ds(target, own), :] = every[i * own : (i + 1) * own]
    every = back_rows[...] * mask
    lanes = every[:, :128]
    for i in range(1, slots * rank // 128):
        lanes = lanes + every[:, i * 128 : (i + 1) * 128]
    turned = lanes.T
    back = turned[:rank]
    for i in range(1, 128 // rank):
        back = back + turned[i * rank : (i + 1) * rank]
    back = back.astype(BF)
    for q in range(tp):
        send_ref[q, :, :share] = normed[:, q * share : (q + 1) * share]
        send_ref[q, :, share:] = back
    send_copy = pltpu.make_async_copy(send_ref, send_hbm, sem.at[2])
    send_copy.start()
    send_copy.wait()


def total_of(refs, i, each):
    total = refs[0][i * each : (i + 1) * each].astype(F32)
    for r in refs[1:]:
        total = total + r[i * each : (i + 1) * each].astype(F32)
    return total.astype(BF)


def sum_kernel(groups, passed, *refs):
    n_in = sum(t for t, _ in groups)
    terms, outs = refs[: n_in], refs[n_in + passed :]
    at, to = 0, 0
    for n, m in groups:
        each = terms[at].shape[0] // m
        for i in range(m):
            if n > 2 and terms[at + 1].shape[0] * (n - 1) == terms[at].shape[0]:
                small = terms[at + 1].shape[0]
                for k in range(each // small):
                    here = terms[at][i * each + k * small : i * each + (k + 1) * small].astype(F32)
                    there = terms[at + 1 + i * (each // small) + k][...].astype(F32)
                    outs[to + i][k * small : (k + 1) * small] = (here + there).astype(BF)
            else:
                outs[to + i][...] = total_of(terms[at : at + n], i, each)
        at, to = at + n, to + m


def mask_kernel(rank, lens_ref, slots_ref, mask_ref):
    mask_ref[...] = mask_by_column(lens_ref, slots_ref, mask_ref.shape[1], rank).astype(BF)


def middle_kernel(rank, mask_ref, recv_ref, down_ref, send_hbm, left_ref, send_ref, sem):
    tp, own, wide = recv_ref.shape
    rows = tp * own
    share = wide - rows
    mask = mask_ref[...].astype(F32)
    normed = recv_ref[:, :, :share].reshape(rows, share)
    every = lax.dot_general(down_ref[...], normed, NT, preferred_element_type=F32) * mask
    slots = every.shape[0] // rank
    low = jnp.sum(every.reshape(slots, rank, rows), axis=0).astype(BF)
    back = jnp.sum(recv_ref[:, :, share:].astype(F32), axis=0).astype(BF).astype(F32)
    left = (mask.reshape(slots, rank, rows) * back[None]).reshape(slots * rank, rows).astype(BF)
    left_ref[...] = left
    term = SCALE * lax.dot_general(left, down_ref[...], TN, preferred_element_type=F32)
    send_ref[:, :, :share] = term.astype(BF).reshape(tp, own, share)
    for q in range(tp):
        send_ref[q, :, share:] = low
    copy = pltpu.make_async_copy(send_ref, send_hbm, sem)
    copy.start()
    copy.wait()


def down_kernel(left_ref, recv_ref, out_ref):
    tp, own, wide = recv_ref.shape
    rows = tp * own
    share = wide - rows
    normed = recv_ref[:, :, :share].reshape(rows, share)
    out_ref[...] = SCALE * jnp.dot(left_ref[...], normed, preferred_element_type=F32)


def up_kernel(rank, mask_ref, recv_ref, cot_ref, out_ref):
    tp, own, wide = recv_ref.shape
    rows = tp * own
    share = wide - rows
    mask = mask_ref[...].astype(F32)
    slots = mask.shape[0] // rank
    low = jnp.sum(recv_ref[:, :, share:].astype(F32), axis=0).astype(BF).astype(F32)
    left = (mask.reshape(slots, rank, rows) * low[None]).reshape(slots * rank, rows).astype(BF)
    out_ref[...] = SCALE * lax.dot_general(cot_ref[...], left, NT, preferred_element_type=F32)


def final_kernel(pieces, recv_ref, tok_ref, *refs):
    out_ref = refs[-1]
    tp, own, _ = recv_ref.shape
    width = tok_ref.shape[1]
    share = width // tp
    chunks = []
    at = 0
    for n in pieces:
        total = refs[at][...].astype(F32)
        for r in refs[at + 1 : at + n]:
            total = total + r[...].astype(F32)
        at += n
        chunks.append(total)
    term = jnp.concatenate([recv_ref[q, :, :share].astype(F32) for q in range(tp)], axis=1)
    grad = jnp.concatenate(chunks, axis=1) + term
    tok = tok_ref[...].astype(F32)
    inv = lax.rsqrt(jnp.mean(tok * tok, axis=1, keepdims=True) + EPS)
    normed = tok * inv
    mean = jnp.mean(grad * normed, axis=1, keepdims=True)
    out_ref[...] = (inv * (grad - normed * mean)).astype(BF)


HBM = pl.BlockSpec(memory_space=pltpu.HBM)


def call(kernel, out, specs, scratch=(), flops=0, nbytes=0, vmem=20, out_specs=None, alias=None):
    return pl.pallas_call(
        kernel,
        out_shape=out,
        in_specs=specs,
        out_specs=jax.tree.map(lambda _: VMEM, out) if out_specs is None else out_specs,
        scratch_shapes=list(scratch),
        input_output_aliases=alias or {},
        cost_estimate=pl.CostEstimate(flops=int(flops), bytes_accessed=int(nbytes), transcendentals=0),
        compiler_params=pltpu.CompilerParams(vmem_limit_bytes=vmem << 20),
    )


def shape(dims, dtype=BF):
    return jax.ShapeDtypeStruct(dims, dtype)


def body(tokens, cotangent, weight, down_maps, up_maps, lengths, slots):
    tp = lax.axis_size("tp")
    me = lax.axis_index("tp").reshape(1)
    own, width = tokens.shape
    rows = own * tp
    count, rank, share = down_maps.shape
    columns = cotangent.shape[0]
    stages = stages_of(tp)
    order = block_order(stages)
    lens = lengths.reshape(1, count)
    slot = slots.reshape(1, count)
    down_flat = down_maps.reshape(count * rank, share)
    weight = pltpu.with_memory_space_constraint(weight, pltpu.HBM)

    half = width * 4 // 8
    block = 1024
    m = len(stages[0])
    each = rows // m
    dma = pltpu.SemaphoreType.DMA
    cotp, *parts_a = call(
        functools.partial(first_kernel, order, own, block),
        [shape((rows, columns))] + [shape((each, half))] * m,
        [SMEM, HBM, HBM],
        scratch=[
            pltpu.VMEM((columns, rows), BF),
            pltpu.VMEM((rows, columns), BF),
            pltpu.VMEM((columns, half), BF),
            dma,
            dma((half // block,)),
        ],
        vmem=20,
        flops=2 * rows * columns * half,
        nbytes=2 * columns * half,
    )(me, cotangent, weight)

    def pairs(m):
        return [(i, i ^ m) for i in range(tp)]

    def exchange(stage, parts):
        return [parts[0]] + [lax.ppermute(part, "tp", pairs(m)) for m, part in zip(stages[stage][1:], parts[1:])]

    def summed(groups, stage_of, passed=()):
        flat = [t for g in groups for t in g]
        cuts = [len(stages[s]) for s in stage_of]
        out = []
        for g, c in zip(groups, cuts):
            out += [shape((g[0].shape[0] // c, g[0].shape[1]))] * c
        n = len(flat)
        res = call(
            functools.partial(sum_kernel, [(len(g), c) for g, c in zip(groups, cuts)], len(passed)),
            out + [shape(x.shape, x.dtype) for x in passed],
            [VMEM] * n + [HBM] * len(passed),
            out_specs=[VMEM] * len(out) + [HBM] * len(passed),
            alias={n + i: len(out) + i for i in range(len(passed))},
            nbytes=4 * sum(x.size for x in flat),
        )(*flat, *passed)
        cut, at = [], 0
        for c in cuts:
            cut.append(list(res[at : at + c]))
            at += c
        return cut, list(res[at:])

    packet = (tp, own, share + rows)
    (send,) = call(
        functools.partial(adapter_kernel, order, rank),
        [shape(packet)],
        [SMEM, VMEM, VMEM, VMEM, HBM, HBM],
        scratch=[
            pltpu.VMEM(packet, BF),
            pltpu.VMEM((own, width), BF),
            pltpu.VMEM((columns, count * rank), BF),
            pltpu.VMEM((rows, count * rank), F32),
            dma((3,)),
        ],
        out_specs=[HBM],
    )(me, lens, slot, cotp, tokens, up_maps)

    last = len(stages) - 1
    held_a = exchange(0, parts_a)
    (cut_a,), _ = summed([held_a], [1])
    (mask,) = call(functools.partial(mask_kernel, rank), [shape((count * rank, rows))], [VMEM, VMEM])(lens, slot)
    recv = lax.all_to_all(send, "tp", split_axis=0, concat_axis=0, tiled=True)
    cut = 2 * len(stages[1])
    parts_b = call(
        functools.partial(second_kernel, half, block),
        [shape((each, width - half))] + [shape((each // cut, width - half))] * cut,
        [VMEM, HBM, HBM],
        scratch=[pltpu.VMEM((columns, width - half), BF), dma(((width - half) // block,))],
    )(cotp, cut_a[0], weight)
    held_b = [parts_b[0]] + [lax.ppermute(part, "tp", pairs(stages[0][1])) for part in parts_b[1:]]
    for stage in range(1, last + 1):
        held_a = exchange(stage, cut_a)
        if stage < last:
            (cut_a, cut_b), _ = summed([held_a, held_b], [stage + 1, stage])
        else:
            (cut_b,), _ = summed([held_b], [stage])
        held_b = exchange(stage, cut_b)
    chunks = [held_a, held_b]

    send2, left = call(
        functools.partial(middle_kernel, rank),
        (shape((tp, own, share + rows)), shape((count * rank, rows))),
        [VMEM] * 3,
        scratch=[pltpu.VMEM((tp, own, share + rows), BF), dma],
        out_specs=[HBM, VMEM],
        flops=4 * rows * share * count * rank,
        nbytes=3 << 20,
    )(mask, recv, down_flat)
    recv2 = lax.all_to_all(send2, "tp", split_axis=0, concat_axis=0, tiled=True)
    down_grad = call(
        down_kernel,
        shape((count * rank, share), F32),
        [VMEM] * 2,
        flops=2 * rows * share * count * rank,
        nbytes=3 << 20,
    )(left, recv)
    up_grad = call(
        functools.partial(up_kernel, rank),
        shape((columns, count * rank), F32),
        [VMEM] * 3,
        flops=2 * rows * columns * count * rank,
        nbytes=3 << 20,
    )(mask, recv2, cotangent)
    flat = [piece for chunk in chunks for piece in chunk]
    grad_tokens = call(
        functools.partial(final_kernel, [len(c) for c in chunks]),
        shape((own, width)),
        [VMEM] * (2 + len(flat)),
        nbytes=2 << 20,
    )(recv2, tokens, *flat)
    return grad_tokens, down_grad.reshape(count, rank, share), up_grad


def solution(mesh):
    in_specs = (
        P(("rep", "tp"), None),
        P("tp", "rep"),
        P("tp", None),
        P(None, None, "tp"),
        P("tp", None),
        P("rep"),
        P(),
    )
    out_specs = (P(("rep", "tp"), None), P("rep", None, "tp"), P("tp", "rep"))
    return jax.shard_map(body, mesh=mesh, in_specs=in_specs, out_specs=out_specs, check_vma=False)
```

```python
import functools

import jax
import jax.numpy as jnp
from jax import lax
from jax.experimental import pallas as pl
from jax.experimental.pallas import tpu as pltpu
from jax.sharding import PartitionSpec as P

SCALE = 2.0
EPS = 1e-06
BF = jnp.bfloat16
F32 = jnp.float32
NT = (((1,), (1,)), ((), ()))
TN = (((0,), (0,)), ((), ()))
VMEM = pl.BlockSpec(memory_space=pltpu.VMEM)
SMEM = pl.BlockSpec(memory_space=pltpu.SMEM)


def stages_of(tp):
    bits = [1 << b for b in range(tp.bit_length() - 1)]
    groups = [bits[:1], bits[1:2]]
    rest = bits[2:]
    groups += [rest[i : i + 2] for i in range(0, len(rest), 2)]
    stages = []
    for group in groups:
        masks = [0]
        for b in group:
            masks = masks + [m | b for m in masks]
        if len(masks) > 1:
            stages.append(masks)
    return stages


def block_order(stages):
    order = [0]
    for masks in stages:
        order = [o | m for o in order for m in masks]
    return order


def iota(shape, dim):
    return lax.broadcasted_iota(jnp.int32, shape, dim)


def membership(lens_ref, slots_ref, rows):
    count = lens_ref.shape[1]
    lens = jnp.broadcast_to(lens_ref[...].astype(F32), (8, count)).astype(BF)
    upto = (iota((count, count), 0) <= iota((count, count), 1)).astype(F32).astype(BF)
    ends = jnp.dot(lens, upto, preferred_element_type=F32)[:1].astype(jnp.int32)
    starts = ends - lens_ref[...]
    position = iota((rows, count), 0)
    member = ((position >= starts) & (position < ends)).astype(F32).astype(BF)
    match = (iota((count, count), 0) == slots_ref[...]).astype(F32).astype(BF)
    return member, match


def mask_by_column(lens_ref, slots_ref, rows, rank):
    member, match = membership(lens_ref, slots_ref, rows)
    chosen = lax.dot_general(match, member, NT, preferred_element_type=F32).astype(BF)
    slots = match.shape[0]
    wide = (iota((slots * rank, slots), 0) // rank == iota((slots * rank, slots), 1)).astype(F32).astype(BF)
    return jnp.dot(wide, chosen, preferred_element_type=F32)


def cast_parts(out, parts):
    each = parts[0].shape[0]
    for i, part in enumerate(parts):
        part[...] = out[i * each : (i + 1) * each].astype(BF)


def fetch_weight(weight_hbm, wbuf, sems, first, block):
    copies = []
    for i in range(wbuf.shape[1] // block):
        copies.append(
            pltpu.make_async_copy(
                weight_hbm.at[:, pl.ds(first + i * block, block)], wbuf.at[:, pl.ds(i * block, block)], sems.at[i]
            )
        )
    return copies


def multiply(cotp, wbuf, copies, block, parts):
    for i, copy in enumerate(copies):
        copy.wait()
        columns = pl.ds(i * block, block)
        out = jnp.dot(cotp, wbuf[:, columns], preferred_element_type=F32)
        at = 0
        for part in parts:
            part[:, columns] = out[at : at + part.shape[0]].astype(BF)
            at += part.shape[0]


def first_kernel(order, own, block, me_ref, cot_hbm, weight_hbm, cotp_ref, *refs):
    *parts, cot, cott, wbuf, sem, sems = refs
    cot_copy = pltpu.make_async_copy(cot_hbm, cot, sem)
    cot_copy.start()
    copies = fetch_weight(weight_hbm, wbuf, sems, 0, block)
    for copy in copies:
        copy.start()
    cot_copy.wait()
    cott[...] = cot[...].astype(F32).T.astype(BF)
    me = me_ref[0]
    for i, mask_bits in enumerate(order):
        source = pl.multiple_of((me ^ mask_bits) * own, own)
        cotp_ref[pl.ds(i * own, own), :] = cott[pl.ds(source, own), :]
    multiply(cotp_ref[...], wbuf, copies, block, parts)


def second_kernel(first, block, cotp_ref, after_hbm, weight_hbm, *refs):
    *parts, wbuf, sems = refs
    copies = fetch_weight(weight_hbm, wbuf, sems, first, block)
    for copy in copies:
        copy.start()
    multiply(cotp_ref[...], wbuf, copies, block, parts)


def adapter_kernel(order, rank, me_ref, lens_ref, slots_ref, cotp_ref, tok_hbm, up_hbm, send_hbm, send_ref, tokv, up, back_rows, sem):
    tp, own, _ = send_ref.shape
    width = tokv.shape[1]
    share = width // tp
    rows = cotp_ref.shape[0]
    tok_copy = pltpu.make_async_copy(tok_hbm, tokv, sem.at[0])
    tok_copy.start()
    up_copy = pltpu.make_async_copy(up_hbm, up, sem.at[1])
    up_copy.start()
    member, match = membership(lens_ref, slots_ref, rows)
    chosen = lax.dot_general(member, match, NT, preferred_element_type=F32).astype(BF)
    slots = match.shape[0]
    wide = (iota((slots, slots * rank), 1) // rank == iota((slots, slots * rank), 0)).astype(F32).astype(BF)
    mask = jnp.dot(chosen, wide, preferred_element_type=F32)
    me = me_ref[0]
    tok_copy.wait()
    tok = tokv[...].astype(F32)
    inv = lax.rsqrt(jnp.mean(tok * tok, axis=1, keepdims=True) + EPS)
    normed = (tok * inv).astype(BF)
    up_copy.wait()
    every = jnp.dot(cotp_ref[...], up[...], preferred_element_type=F32)
    for i, mask_bits in enumerate(order):
        target = pl.multiple_of((me ^ mask_bits) * own, own)
        back_rows[pl.ds(target, own), :] = every[i * own : (i + 1) * own]
    every = back_rows[...] * mask
    lanes = every[:, :128]
    for i in range(1, slots * rank // 128):
        lanes = lanes + every[:, i * 128 : (i + 1) * 128]
    turned = lanes.T
    back = turned[:rank]
    for i in range(1, 128 // rank):
        back = back + turned[i * rank : (i + 1) * rank]
    back = back.astype(BF)
    for q in range(tp):
        send_ref[q, :, :share] = normed[:, q * share : (q + 1) * share]
        send_ref[q, :, share:] = back
    send_copy = pltpu.make_async_copy(send_ref, send_hbm, sem.at[2])
    send_copy.start()
    send_copy.wait()


def total_of(refs, i, each):
    total = refs[0][i * each : (i + 1) * each].astype(F32)
    for r in refs[1:]:
        total = total + r[i * each : (i + 1) * each].astype(F32)
    return total.astype(BF)


def sum_kernel(groups, passed, *refs):
    n_in = sum(t for t, _ in groups)
    terms, outs = refs[: n_in], refs[n_in + passed :]
    at, to = 0, 0
    for n, m in groups:
        each = terms[at].shape[0] // m
        for i in range(m):
            if n > 2 and terms[at + 1].shape[0] * (n - 1) == terms[at].shape[0]:
                small = terms[at + 1].shape[0]
                for k in range(each // small):
                    here = terms[at][i * each + k * small : i * each + (k + 1) * small].astype(F32)
                    there = terms[at + 1 + i * (each // small) + k][...].astype(F32)
                    outs[to + i][k * small : (k + 1) * small] = (here + there).astype(BF)
            else:
                outs[to + i][...] = total_of(terms[at : at + n], i, each)
        at, to = at + n, to + m


def mask_kernel(rank, lens_ref, slots_ref, mask_ref):
    mask_ref[...] = mask_by_column(lens_ref, slots_ref, mask_ref.shape[1], rank).astype(BF)


def middle_kernel(rank, mask_ref, recv_ref, down_hbm, send_hbm, back_ref, send_ref, down_ref, sem):
    fetch = pltpu.make_async_copy(down_hbm, down_ref, sem)
    fetch.start()
    tp, own, wide = recv_ref.shape
    rows = tp * own
    share = wide - rows
    mask = mask_ref[...].astype(F32)
    normed = recv_ref[:, :, :share].reshape(rows, share)
    slots = mask.shape[0] // rank
    back = jnp.sum(recv_ref[:, :, share:].astype(F32), axis=0).astype(BF).astype(F32)
    left = (mask.reshape(slots, rank, rows) * back[None]).reshape(slots * rank, rows).astype(BF)
    back_ref[...] = back
    fetch.wait()
    every = lax.dot_general(down_ref[...], normed, NT, preferred_element_type=F32) * mask
    low = jnp.sum(every.reshape(slots, rank, rows), axis=0).astype(BF)
    term = SCALE * lax.dot_general(left, down_ref[...], TN, preferred_element_type=F32)
    send_ref[:, :, :share] = term.astype(BF).reshape(tp, own, share)
    for q in range(tp):
        send_ref[q, :, share:] = low
    copy = pltpu.make_async_copy(send_ref, send_hbm, sem)
    copy.start()
    copy.wait()


def down_kernel(rank, mask_ref, back_ref, recv_ref, out_ref):
    tp, own, wide = recv_ref.shape
    rows = tp * own
    share = wide - rows
    normed = recv_ref[:, :, :share].reshape(rows, share)
    mask = mask_ref[...].astype(F32)
    slots = mask.shape[0] // rank
    left = (mask.reshape(slots, rank, rows) * back_ref[...][None]).reshape(slots * rank, rows).astype(BF)
    out_ref[...] = SCALE * jnp.dot(left, normed, preferred_element_type=F32)


def up_kernel(rank, mask_ref, recv_ref, cot_ref, out_ref):
    tp, own, wide = recv_ref.shape
    rows = tp * own
    share = wide - rows
    mask = mask_ref[...].astype(F32)
    slots = mask.shape[0] // rank
    low = jnp.sum(recv_ref[:, :, share:].astype(F32), axis=0).astype(BF).astype(F32)
    left = (mask.reshape(slots, rank, rows) * low[None]).reshape(slots * rank, rows).astype(BF)
    out_ref[...] = SCALE * lax.dot_general(cot_ref[...], left, NT, preferred_element_type=F32)


def final_kernel(pieces, recv_ref, tok_ref, *refs):
    out_ref = refs[-1]
    tp, own, _ = recv_ref.shape
    width = tok_ref.shape[1]
    share = width // tp
    chunks = []
    at = 0
    for n in pieces:
        total = refs[at][...].astype(F32)
        for r in refs[at + 1 : at + n]:
            total = total + r[...].astype(F32)
        at += n
        chunks.append(total)
    term = jnp.concatenate([recv_ref[q, :, :share].astype(F32) for q in range(tp)], axis=1)
    grad = jnp.concatenate(chunks, axis=1) + term
    tok = tok_ref[...].astype(F32)
    inv = lax.rsqrt(jnp.mean(tok * tok, axis=1, keepdims=True) + EPS)
    normed = tok * inv
    mean = jnp.mean(grad * normed, axis=1, keepdims=True)
    out_ref[...] = (inv * (grad - normed * mean)).astype(BF)


HBM = pl.BlockSpec(memory_space=pltpu.HBM)


def call(kernel, out, specs, scratch=(), flops=0, nbytes=0, vmem=20, out_specs=None, alias=None):
    return pl.pallas_call(
        kernel,
        out_shape=out,
        in_specs=specs,
        out_specs=jax.tree.map(lambda _: VMEM, out) if out_specs is None else out_specs,
        scratch_shapes=list(scratch),
        input_output_aliases=alias or {},
        cost_estimate=pl.CostEstimate(flops=int(flops), bytes_accessed=int(nbytes), transcendentals=0),
        compiler_params=pltpu.CompilerParams(vmem_limit_bytes=vmem << 20),
    )


def shape(dims, dtype=BF):
    return jax.ShapeDtypeStruct(dims, dtype)


def body(tokens, cotangent, weight, down_maps, up_maps, lengths, slots):
    tp = lax.axis_size("tp")
    me = lax.axis_index("tp").reshape(1)
    own, width = tokens.shape
    rows = own * tp
    count, rank, share = down_maps.shape
    columns = cotangent.shape[0]
    stages = stages_of(tp)
    order = block_order(stages)
    lens = lengths.reshape(1, count)
    slot = slots.reshape(1, count)
    down_flat = down_maps.reshape(count * rank, share)
    weight = pltpu.with_memory_space_constraint(weight, pltpu.HBM)

    half = width * 4 // 8
    block = 1024
    m = len(stages[0])
    each = rows // m
    dma = pltpu.SemaphoreType.DMA
    cotp, *parts_a = call(
        functools.partial(first_kernel, order, own, block),
        [shape((rows, columns))] + [shape((each, half))] * m,
        [SMEM, HBM, HBM],
        scratch=[
            pltpu.VMEM((columns, rows), BF),
            pltpu.VMEM((rows, columns), BF),
            pltpu.VMEM((columns, half), BF),
            dma,
            dma((half // block,)),
        ],
        vmem=20,
        flops=2 * rows * columns * half,
        nbytes=2 * columns * half,
    )(me, cotangent, weight)

    def pairs(m):
        return [(i, i ^ m) for i in range(tp)]

    def exchange(stage, parts):
        return [parts[0]] + [lax.ppermute(part, "tp", pairs(m)) for m, part in zip(stages[stage][1:], parts[1:])]

    def summed(groups, stage_of, passed=()):
        flat = [t for g in groups for t in g]
        cuts = [len(stages[s]) for s in stage_of]
        out = []
        for g, c in zip(groups, cuts):
            out += [shape((g[0].shape[0] // c, g[0].shape[1]))] * c
        n = len(flat)
        res = call(
            functools.partial(sum_kernel, [(len(g), c) for g, c in zip(groups, cuts)], len(passed)),
            out + [shape(x.shape, x.dtype) for x in passed],
            [VMEM] * n + [HBM] * len(passed),
            out_specs=[VMEM] * len(out) + [HBM] * len(passed),
            alias={n + i: len(out) + i for i in range(len(passed))},
            nbytes=4 * sum(x.size for x in flat),
        )(*flat, *passed)
        cut, at = [], 0
        for c in cuts:
            cut.append(list(res[at : at + c]))
            at += c
        return cut, list(res[at:])

    packet = (tp, own, share + rows)
    (send,) = call(
        functools.partial(adapter_kernel, order, rank),
        [shape(packet)],
        [SMEM, VMEM, VMEM, VMEM, HBM, HBM],
        scratch=[
            pltpu.VMEM(packet, BF),
            pltpu.VMEM((own, width), BF),
            pltpu.VMEM((columns, count * rank), BF),
            pltpu.VMEM((rows, count * rank), F32),
            dma((3,)),
        ],
        out_specs=[HBM],
    )(me, lens, slot, cotp, tokens, up_maps)

    last = len(stages) - 1
    held_a = exchange(0, parts_a)
    total = sum(x.astype(F32) for x in held_a).astype(BF)
    cut_a = jnp.split(total, len(stages[1]), axis=0)
    (mask,) = call(functools.partial(mask_kernel, rank), [shape((count * rank, rows))], [VMEM, VMEM])(lens, slot)
    recv = lax.all_to_all(send, "tp", split_axis=0, concat_axis=0, tiled=True)
    cut = 2 * len(stages[1])
    parts_b = call(
        functools.partial(second_kernel, half, block),
        [shape((each, width - half))] + [shape((each // cut, width - half))] * cut,
        [VMEM, HBM, HBM],
        scratch=[pltpu.VMEM((columns, width - half), BF), dma(((width - half) // block,))],
    )(cotp, cut_a[0], weight)
    held_b = [parts_b[0]] + [lax.ppermute(part, "tp", pairs(stages[0][1])) for part in parts_b[1:]]
    for stage in range(1, last + 1):
        held_a = exchange(stage, cut_a)
        if stage < last:
            (cut_a, cut_b), _ = summed([held_a, held_b], [stage + 1, stage])
        else:
            (cut_b,), _ = summed([held_b], [stage])
        held_b = exchange(stage, cut_b)
    chunks = [held_a, held_b]

    send2, back = call(
        functools.partial(middle_kernel, rank),
        (shape((tp, own, share + rows)), shape((rank, rows), F32)),
        [VMEM, VMEM, HBM],
        scratch=[pltpu.VMEM((tp, own, share + rows), BF), pltpu.VMEM((count * rank, share), BF), dma],
        out_specs=[HBM, VMEM],
        flops=4 * rows * share * count * rank,
        nbytes=3 << 20,
    )(mask, recv, pltpu.with_memory_space_constraint(down_flat, pltpu.HBM))
    recv2 = lax.all_to_all(send2, "tp", split_axis=0, concat_axis=0, tiled=True)
    down_grad = call(
        functools.partial(down_kernel, rank),
        shape((count * rank, share), F32),
        [VMEM] * 3,
        flops=2 * rows * share * count * rank,
        nbytes=3 << 20,
    )(mask, back, recv)
    up_grad = call(
        functools.partial(up_kernel, rank),
        shape((columns, count * rank), F32),
        [VMEM] * 3,
        flops=2 * rows * columns * count * rank,
        nbytes=3 << 20,
    )(mask, recv2, cotangent)
    flat = [piece for chunk in chunks for piece in chunk]
    grad_tokens = call(
        functools.partial(final_kernel, [len(c) for c in chunks]),
        shape((own, width)),
        [VMEM] * (2 + len(flat)),
        nbytes=2 << 20,
    )(recv2, tokens, *flat)
    return grad_tokens, down_grad.reshape(count, rank, share), up_grad


def solution(mesh):
    in_specs = (
        P(("rep", "tp"), None),
        P("tp", "rep"),
        P("tp", None),
        P(None, None, "tp"),
        P("tp", None),
        P("rep"),
        P(),
    )
    out_specs = (P(("rep", "tp"), None), P("rep", None, "tp"), P("tp", "rep"))
    return jax.shard_map(body, mesh=mesh, in_specs=in_specs, out_specs=out_specs, check_vma=False)
```

```python
import functools

import jax
import jax.numpy as jnp
from jax import lax
from jax.experimental import pallas as pl
from jax.experimental.pallas import tpu as pltpu
from jax.sharding import PartitionSpec as P

SCALE = 2.0
EPS = 1e-06
BF = jnp.bfloat16
F32 = jnp.float32
NT = (((1,), (1,)), ((), ()))
TN = (((0,), (0,)), ((), ()))
VMEM = pl.BlockSpec(memory_space=pltpu.VMEM)
SMEM = pl.BlockSpec(memory_space=pltpu.SMEM)


def stages_of(tp):
    bits = [1 << b for b in range(tp.bit_length() - 1)]
    groups = [bits[:1], bits[1:2]]
    rest = bits[2:]
    groups += [rest[i : i + 2] for i in range(0, len(rest), 2)]
    stages = []
    for group in groups:
        masks = [0]
        for b in group:
            masks = masks + [m | b for m in masks]
        if len(masks) > 1:
            stages.append(masks)
    return stages


def block_order(stages):
    order = [0]
    for masks in stages:
        order = [o | m for o in order for m in masks]
    return order


def iota(shape, dim):
    return lax.broadcasted_iota(jnp.int32, shape, dim)


def membership(lens_ref, slots_ref, rows):
    count = lens_ref.shape[1]
    lens = jnp.broadcast_to(lens_ref[...].astype(F32), (8, count)).astype(BF)
    upto = (iota((count, count), 0) <= iota((count, count), 1)).astype(F32).astype(BF)
    ends = jnp.dot(lens, upto, preferred_element_type=F32)[:1].astype(jnp.int32)
    starts = ends - lens_ref[...]
    position = iota((rows, count), 0)
    member = ((position >= starts) & (position < ends)).astype(F32).astype(BF)
    match = (iota((count, count), 0) == slots_ref[...]).astype(F32).astype(BF)
    return member, match


def mask_by_column(lens_ref, slots_ref, rows, rank):
    member, match = membership(lens_ref, slots_ref, rows)
    chosen = lax.dot_general(match, member, NT, preferred_element_type=F32).astype(BF)
    slots = match.shape[0]
    wide = (iota((slots * rank, slots), 0) // rank == iota((slots * rank, slots), 1)).astype(F32).astype(BF)
    return jnp.dot(wide, chosen, preferred_element_type=F32)


def cast_parts(out, parts):
    each = parts[0].shape[0]
    for i, part in enumerate(parts):
        part[...] = out[i * each : (i + 1) * each].astype(BF)


def fetch_weight(weight_hbm, wbuf, sems, first, block):
    copies = []
    for i in range(wbuf.shape[1] // block):
        copies.append(
            pltpu.make_async_copy(
                weight_hbm.at[:, pl.ds(first + i * block, block)], wbuf.at[:, pl.ds(i * block, block)], sems.at[i]
            )
        )
    return copies


def multiply(cotp, wbuf, copies, block, parts):
    for i, copy in enumerate(copies):
        copy.wait()
        columns = pl.ds(i * block, block)
        out = jnp.dot(cotp, wbuf[:, columns], preferred_element_type=F32)
        at = 0
        for part in parts:
            part[:, columns] = out[at : at + part.shape[0]].astype(BF)
            at += part.shape[0]


def first_kernel(order, own, block, me_ref, cot_hbm, weight_hbm, cotp_ref, *refs):
    *parts, cot, cott, wbuf, sem, sems = refs
    cot_copy = pltpu.make_async_copy(cot_hbm, cot, sem)
    cot_copy.start()
    copies = fetch_weight(weight_hbm, wbuf, sems, 0, block)
    for copy in copies:
        copy.start()
    cot_copy.wait()
    cott[...] = cot[...].astype(F32).T.astype(BF)
    me = me_ref[0]
    for i, mask_bits in enumerate(order):
        source = pl.multiple_of((me ^ mask_bits) * own, own)
        cotp_ref[pl.ds(i * own, own), :] = cott[pl.ds(source, own), :]
    multiply(cotp_ref[...], wbuf, copies, block, parts)


def second_kernel(first, block, cotp_ref, after_hbm, weight_hbm, *refs):
    *parts, wbuf, sems = refs
    copies = fetch_weight(weight_hbm, wbuf, sems, first, block)
    for copy in copies:
        copy.start()
    multiply(cotp_ref[...], wbuf, copies, block, parts)


def adapter_kernel(order, rank, me_ref, lens_ref, slots_ref, cotp_ref, tok_hbm, up_hbm, send_hbm, send_ref, tokv, up, back_rows, sem):
    tp, own, _ = send_ref.shape
    width = tokv.shape[1]
    share = width // tp
    rows = cotp_ref.shape[0]
    tok_copy = pltpu.make_async_copy(tok_hbm, tokv, sem.at[0])
    tok_copy.start()
    up_copy = pltpu.make_async_copy(up_hbm, up, sem.at[1])
    up_copy.start()
    member, match = membership(lens_ref, slots_ref, rows)
    chosen = lax.dot_general(member, match, NT, preferred_element_type=F32).astype(BF)
    slots = match.shape[0]
    wide = (iota((slots, slots * rank), 1) // rank == iota((slots, slots * rank), 0)).astype(F32).astype(BF)
    mask = jnp.dot(chosen, wide, preferred_element_type=F32)
    me = me_ref[0]
    tok_copy.wait()
    tok = tokv[...].astype(F32)
    inv = lax.rsqrt(jnp.mean(tok * tok, axis=1, keepdims=True) + EPS)
    normed = (tok * inv).astype(BF)
    up_copy.wait()
    every = jnp.dot(cotp_ref[...], up[...], preferred_element_type=F32)
    for i, mask_bits in enumerate(order):
        target = pl.multiple_of((me ^ mask_bits) * own, own)
        back_rows[pl.ds(target, own), :] = every[i * own : (i + 1) * own]
    every = back_rows[...] * mask
    lanes = every[:, :128]
    for i in range(1, slots * rank // 128):
        lanes = lanes + every[:, i * 128 : (i + 1) * 128]
    turned = lanes.T
    back = turned[:rank]
    for i in range(1, 128 // rank):
        back = back + turned[i * rank : (i + 1) * rank]
    back = back.astype(BF)
    for q in range(tp):
        send_ref[q, :, :share] = normed[:, q * share : (q + 1) * share]
        send_ref[q, :, share:] = back
    send_copy = pltpu.make_async_copy(send_ref, send_hbm, sem.at[2])
    send_copy.start()
    send_copy.wait()


def total_of(refs, i, each):
    total = refs[0][i * each : (i + 1) * each].astype(F32)
    for r in refs[1:]:
        total = total + r[i * each : (i + 1) * each].astype(F32)
    return total.astype(BF)


def sum_kernel(groups, passed, *refs):
    n_in = sum(t for t, _ in groups)
    terms, outs = refs[: n_in], refs[n_in + passed :]
    at, to = 0, 0
    for n, m in groups:
        each = terms[at].shape[0] // m
        for i in range(m):
            if n > 2 and terms[at + 1].shape[0] * (n - 1) == terms[at].shape[0]:
                small = terms[at + 1].shape[0]
                for k in range(each // small):
                    here = terms[at][i * each + k * small : i * each + (k + 1) * small].astype(F32)
                    there = terms[at + 1 + i * (each // small) + k][...].astype(F32)
                    outs[to + i][k * small : (k + 1) * small] = (here + there).astype(BF)
            else:
                outs[to + i][...] = total_of(terms[at : at + n], i, each)
        at, to = at + n, to + m


def mask_kernel(rank, lens_ref, slots_ref, mask_ref):
    mask_ref[...] = mask_by_column(lens_ref, slots_ref, mask_ref.shape[1], rank).astype(BF)


def middle_kernel(rank, mask_ref, recv_ref, down_hbm, send_hbm, back_ref, send_ref, down_ref, sem):
    fetch = pltpu.make_async_copy(down_hbm, down_ref, sem)
    fetch.start()
    tp, own, wide = recv_ref.shape
    rows = tp * own
    share = wide - rows
    mask = mask_ref[...].astype(F32)
    normed = recv_ref[:, :, :share].reshape(rows, share)
    slots = mask.shape[0] // rank
    back = jnp.sum(recv_ref[:, :, share:].astype(F32), axis=0).astype(BF).astype(F32)
    left = (mask.reshape(slots, rank, rows) * back[None]).reshape(slots * rank, rows).astype(BF)
    back_ref[...] = back
    fetch.wait()
    every = lax.dot_general(down_ref[...], normed, NT, preferred_element_type=F32) * mask
    low = jnp.sum(every.reshape(slots, rank, rows), axis=0).astype(BF)
    term = SCALE * lax.dot_general(left, down_ref[...], TN, preferred_element_type=F32)
    send_ref[:, :, :share] = term.astype(BF).reshape(tp, own, share)
    for q in range(tp):
        send_ref[q, :, share:] = low
    copy = pltpu.make_async_copy(send_ref, send_hbm, sem)
    copy.start()
    copy.wait()


def down_kernel(rank, mask_ref, back_ref, recv_ref, out_ref):
    tp, own, wide = recv_ref.shape
    rows = tp * own
    share = wide - rows
    normed = recv_ref[:, :, :share].reshape(rows, share)
    mask = mask_ref[...].astype(F32)
    slots = mask.shape[0] // rank
    left = (mask.reshape(slots, rank, rows) * back_ref[...][None]).reshape(slots * rank, rows).astype(BF)
    out_ref[...] = SCALE * jnp.dot(left, normed, preferred_element_type=F32)


def up_kernel(rank, mask_ref, recv_ref, cot_ref, out_ref):
    tp, own, wide = recv_ref.shape
    rows = tp * own
    share = wide - rows
    mask = mask_ref[...].astype(F32)
    slots = mask.shape[0] // rank
    low = jnp.sum(recv_ref[:, :, share:].astype(F32), axis=0).astype(BF).astype(F32)
    left = (mask.reshape(slots, rank, rows) * low[None]).reshape(slots * rank, rows).astype(BF)
    out_ref[...] = SCALE * lax.dot_general(cot_ref[...], left, NT, preferred_element_type=F32)


def final_kernel(pieces, recv_ref, tok_ref, *refs):
    out_ref = refs[-1]
    tp, own, _ = recv_ref.shape
    width = tok_ref.shape[1]
    share = width // tp
    chunks = []
    at = 0
    for n in pieces:
        total = refs[at][...].astype(F32)
        for r in refs[at + 1 : at + n]:
            total = total + r[...].astype(F32)
        at += n
        chunks.append(total)
    term = jnp.concatenate([recv_ref[q, :, :share].astype(F32) for q in range(tp)], axis=1)
    grad = jnp.concatenate(chunks, axis=1) + term
    tok = tok_ref[...].astype(F32)
    inv = lax.rsqrt(jnp.mean(tok * tok, axis=1, keepdims=True) + EPS)
    normed = tok * inv
    mean = jnp.mean(grad * normed, axis=1, keepdims=True)
    out_ref[...] = (inv * (grad - normed * mean)).astype(BF)


HBM = pl.BlockSpec(memory_space=pltpu.HBM)


def call(kernel, out, specs, scratch=(), flops=0, nbytes=0, vmem=20, out_specs=None, alias=None):
    return pl.pallas_call(
        kernel,
        out_shape=out,
        in_specs=specs,
        out_specs=jax.tree.map(lambda _: VMEM, out) if out_specs is None else out_specs,
        scratch_shapes=list(scratch),
        input_output_aliases=alias or {},
        cost_estimate=pl.CostEstimate(flops=int(flops), bytes_accessed=int(nbytes), transcendentals=0),
        compiler_params=pltpu.CompilerParams(vmem_limit_bytes=vmem << 20),
    )


def shape(dims, dtype=BF):
    return jax.ShapeDtypeStruct(dims, dtype)


def body(tokens, cotangent, weight, down_maps, up_maps, lengths, slots):
    tp = lax.axis_size("tp")
    me = lax.axis_index("tp").reshape(1)
    own, width = tokens.shape
    rows = own * tp
    count, rank, share = down_maps.shape
    columns = cotangent.shape[0]
    stages = stages_of(tp)
    order = block_order(stages)
    lens = lengths.reshape(1, count)
    slot = slots.reshape(1, count)
    down_flat = down_maps.reshape(count * rank, share)
    weight = pltpu.with_memory_space_constraint(weight, pltpu.HBM)

    half = width * 4 // 8
    block = 1024
    m = len(stages[0])
    each = rows // m
    dma = pltpu.SemaphoreType.DMA
    cotp, *parts_a = call(
        functools.partial(first_kernel, order, own, block),
        [shape((rows, columns))] + [shape((each, half))] * m,
        [SMEM, HBM, HBM],
        scratch=[
            pltpu.VMEM((columns, rows), BF),
            pltpu.VMEM((rows, columns), BF),
            pltpu.VMEM((columns, half), BF),
            dma,
            dma((half // block,)),
        ],
        vmem=20,
        flops=2 * rows * columns * half,
        nbytes=2 * columns * half,
    )(me, cotangent, weight)

    def pairs(m):
        return [(i, i ^ m) for i in range(tp)]

    def exchange(stage, parts):
        return [parts[0]] + [lax.ppermute(part, "tp", pairs(m)) for m, part in zip(stages[stage][1:], parts[1:])]

    def summed(groups, stage_of, passed=()):
        flat = [t for g in groups for t in g]
        cuts = [len(stages[s]) for s in stage_of]
        out = []
        for g, c in zip(groups, cuts):
            out += [shape((g[0].shape[0] // c, g[0].shape[1]))] * c
        n = len(flat)
        res = call(
            functools.partial(sum_kernel, [(len(g), c) for g, c in zip(groups, cuts)], len(passed)),
            out + [shape(x.shape, x.dtype) for x in passed],
            [VMEM] * n + [HBM] * len(passed),
            out_specs=[VMEM] * len(out) + [HBM] * len(passed),
            alias={n + i: len(out) + i for i in range(len(passed))},
            nbytes=4 * sum(x.size for x in flat),
        )(*flat, *passed)
        cut, at = [], 0
        for c in cuts:
            cut.append(list(res[at : at + c]))
            at += c
        return cut, list(res[at:])

    packet = (tp, own, share + rows)
    (send,) = call(
        functools.partial(adapter_kernel, order, rank),
        [shape(packet)],
        [SMEM, VMEM, VMEM, VMEM, HBM, HBM],
        scratch=[
            pltpu.VMEM(packet, BF),
            pltpu.VMEM((own, width), BF),
            pltpu.VMEM((columns, count * rank), BF),
            pltpu.VMEM((rows, count * rank), F32),
            dma((3,)),
        ],
        out_specs=[HBM],
    )(me, lens, slot, cotp, tokens, up_maps)

    last = len(stages) - 1
    held_a = exchange(0, parts_a)
    rows_cut = each // len(stages[1])
    cut_a = [
        sum(x[i * rows_cut : (i + 1) * rows_cut].astype(F32) for x in held_a).astype(BF) for i in range(len(stages[1]))
    ]
    (mask,) = call(functools.partial(mask_kernel, rank), [shape((count * rank, rows))], [VMEM, VMEM])(lens, slot)
    recv = lax.all_to_all(send, "tp", split_axis=0, concat_axis=0, tiled=True)
    cut = 2 * len(stages[1])
    parts_b = call(
        functools.partial(second_kernel, half, block),
        [shape((each, width - half))] + [shape((each // cut, width - half))] * cut,
        [VMEM, HBM, HBM],
        scratch=[pltpu.VMEM((columns, width - half), BF), dma(((width - half) // block,))],
    )(cotp, cut_a[0], weight)
    held_b = [parts_b[0]] + [lax.ppermute(part, "tp", pairs(stages[0][1])) for part in parts_b[1:]]
    for stage in range(1, last + 1):
        held_a = exchange(stage, cut_a)
        if stage < last:
            (cut_a, cut_b), _ = summed([held_a, held_b], [stage + 1, stage])
        else:
            (cut_b,), _ = summed([held_b], [stage])
        held_b = exchange(stage, cut_b)
    chunks = [held_a, held_b]

    send2, back = call(
        functools.partial(middle_kernel, rank),
        (shape((tp, own, share + rows)), shape((rank, rows), F32)),
        [VMEM, VMEM, HBM],
        scratch=[pltpu.VMEM((tp, own, share + rows), BF), pltpu.VMEM((count * rank, share), BF), dma],
        out_specs=[HBM, VMEM],
        flops=4 * rows * share * count * rank,
        nbytes=3 << 20,
    )(mask, recv, pltpu.with_memory_space_constraint(down_flat, pltpu.HBM))
    recv2 = lax.all_to_all(send2, "tp", split_axis=0, concat_axis=0, tiled=True)
    down_grad = call(
        functools.partial(down_kernel, rank),
        shape((count * rank, share), F32),
        [VMEM] * 3,
        flops=2 * rows * share * count * rank,
        nbytes=3 << 20,
    )(mask, back, recv)
    up_grad = call(
        functools.partial(up_kernel, rank),
        shape((columns, count * rank), F32),
        [VMEM] * 3,
        flops=2 * rows * columns * count * rank,
        nbytes=3 << 20,
    )(mask, recv2, cotangent)
    flat = [piece for chunk in chunks for piece in chunk]
    grad_tokens = call(
        functools.partial(final_kernel, [len(c) for c in chunks]),
        shape((own, width)),
        [VMEM] * (2 + len(flat)),
        nbytes=2 << 20,
    )(recv2, tokens, *flat)
    return grad_tokens, down_grad.reshape(count, rank, share), up_grad


def solution(mesh):
    in_specs = (
        P(("rep", "tp"), None),
        P("tp", "rep"),
        P("tp", None),
        P(None, None, "tp"),
        P("tp", None),
        P("rep"),
        P(),
    )
    out_specs = (P(("rep", "tp"), None), P("rep", None, "tp"), P("tp", "rep"))
    return jax.shard_map(body, mesh=mesh, in_specs=in_specs, out_specs=out_specs, check_vma=False)
```
